256 devices in a mesh: row: 32 (over z, x), col: 8 (over y, core).
Axes of the slice: x: 4, y: 4, z: 8, core: 2. Of those that a mesh axis runs over, the one named last changes fastest.
Arguments:
- panel: float32 [32768, 2048], P('row', 'col'), as said below
- rhs: float32 [32768, 2048], P('row', 'col'), may hold values from -6 to 6
Outputs:
- trailing: float32 [32768, 2048], P('row', 'col')
- solution: float32 [2048, 2048], P(None, 'col')
The draws below stay inside these ranges and needn't reach their ends.
Inputs may be any that keep to these rules, and one draw needn't show every extreme that they name: Rows of panel are ordered as in the reference program. The blocks L0 and L1 are lower triangular with diagonal entries between 1 and 2; P[0, 0] is zero in the columns of block 1.
All inputs are finite; a program needn't handle non-finite values.
Results may differ from the reference program's by a relative error of at most 0.000094.
Values sent between devices are 32-bit elements; how exact they have to be, the bound alone decides.
No kernel may reach another device: no remote copies, remote signals or barrier semaphores. Data moves between devices by JAX's collectives and lax.ppermute only.
A program may use at most 128 MiB of HBM per device.

```python
import math
import jax
import jax.numpy as jnp
from jax import lax

NB = 1024
NRHS = 2048
BLK_DEV = 1
ROWS = 32768
N_ROW = 32


def draw_panel(key, part):
    key = jax.random.fold_in(key, 7)
    noise_key, diag_key = jax.random.split(key)
    shape = (ROWS, 2 * NB)
    noise = jax.random.normal(noise_key, shape, jnp.float32)
    diag_vals = jax.random.uniform(diag_key, shape, jnp.float32, 1.0, 2.0)
    row_pos = jnp.arange(ROWS, dtype=jnp.int32)[:, None]
    col_pos = jnp.arange(2 * NB, dtype=jnp.int32)[None, :]
    device = row_pos // (BLK_DEV * NB)
    slot = row_pos // NB % BLK_DEV
    inner_row = row_pos % NB
    col_block = col_pos // NB
    inner_col = col_pos % NB
    on_diag = (slot == 0) & (device == col_block)
    above = (slot == 0) & (device < col_block)
    lower_part = jnp.where(inner_col == inner_row, diag_vals, jnp.where(inner_col < inner_row, noise * (0.5 / math.sqrt(NB)), 0.0))
    general = noise * (1.0 / math.sqrt(2 * NB))
    return jnp.where(on_diag, lower_part, jnp.where(above, 0.0, general)).astype(jnp.float32)


def block_levels(own_key, extent, shards, low, top_value):
    def one(dim, blocks):
        draws = jax.random.uniform(jax.random.fold_in(jax.random.fold_in(own_key, 6), dim), (blocks,), jnp.float32, low / len(shards), top_value / len(shards))
        return jnp.repeat(jnp.exp(draws), extent[dim] // blocks).reshape((-1,) + (1,) * (len(extent) - dim - 1))

    gain = one(*shards[0])
    for cut in shards[1:]:
        gain = gain * one(*cut)
    return gain


def normal_values(own_key, shape, width, most, shards=(), kind=jnp.bfloat16):
    result = jax.random.normal(own_key, shape, jnp.float32) * width
    if len(shards) > 0:
        result = block_levels(own_key, shape, shards, -0.22, 0.18) * result
    return jnp.clip(result, min=-most, max=most).astype(kind)


def setup_inputs(seed: int = 0) -> dict:
    seeds = jax.random.split(jax.random.key(seed), 3)
    return {
        "panel": draw_panel(jax.random.fold_in(seeds[2], 71), 0),
        "rhs": normal_values(seeds[1], (ROWS, NRHS), 1.0, 6.0, ((0, 32), (1, 8)), jnp.float32),
    }


def tri_solve(matrix, targets):
    return jax.scipy.linalg.solve_triangular(matrix, targets, lower=True)

def subtract(targets, blocks, solved):
    return targets - jnp.einsum('gsik,kn->gsin', blocks, solved, precision=lax.Precision.HIGHEST)

def reference(panel, rhs):
    blocks = panel.reshape(N_ROW, BLK_DEV, NB, 2 * NB)
    targets = rhs.reshape(N_ROW, BLK_DEV, NB, NRHS)
    solved_one = tri_solve(blocks[0, 0, :, :NB], targets[0, 0])
    targets = subtract(targets, blocks[:, :, :, :NB], solved_one)
    solved_two = tri_solve(blocks[1, 0, :, NB:], targets[1, 0])
    targets = subtract(targets, blocks[:, :, :, NB:], solved_two)
    targets = targets.at[0, 0].set(jnp.float32(0.0)).at[1, 0].set(jnp.float32(0.0))
    return (targets.reshape(ROWS, NRHS), jnp.concatenate([solved_one, solved_two], axis=0))
```

```python
import functools

import jax
import jax.numpy as jnp
from jax import lax
from jax.experimental import pallas as pl
from jax.experimental.pallas import tpu as pltpu
from jax.sharding import PartitionSpec as P

NB = 1024
Q = 256
PARTS = 4
XS = 4
ZS = 8
COLS = 8
F32 = jnp.float32
BF16 = jnp.bfloat16


def halves(value):
    high = value.astype(BF16)
    return high, (value - high.astype(F32)).astype(BF16)


def product(left, right):
    dot = functools.partial(jnp.dot, preferred_element_type=F32)
    return dot(left[0], right[0]) + (dot(left[0], right[1]) + dot(left[1], right[0]))


def invert_kernel(flag_ref, block_ref, out_ref):
    @pl.when(flag_ref[0] == 1)
    def _():
        rows = lax.broadcasted_iota(jnp.int32, (Q, Q), 0)
        cols = lax.broadcasted_iota(jnp.int32, (Q, Q), 1)
        block = block_ref[...]
        inverse = jnp.where(rows == cols, 1.0 / jnp.where(rows == cols, block, 1.0), 0.0)
        level = 0
        while (1 << level) < Q:
            pair = (rows >> (level + 1)) == (cols >> (level + 1))
            below = pair & (((rows >> level) & 1) == 1) & (((cols >> level) & 1) == 0)
            parts = halves(inverse)
            inner = product(halves(jnp.where(below, block, 0.0)), parts)
            inverse = inverse - product(parts, halves(inner))
            level += 1
        out_ref[...] = inverse


def invert(flag, block):
    return pl.pallas_call(
        invert_kernel,
        out_shape=jax.ShapeDtypeStruct((Q, Q), F32),
        in_specs=[pl.BlockSpec(memory_space=pltpu.SMEM), pl.BlockSpec(memory_space=pltpu.VMEM)],
        out_specs=pl.BlockSpec(memory_space=pltpu.VMEM),
        compiler_params=pltpu.CompilerParams(vmem_limit_bytes=32 << 20),
        name="invert",
    )(flag, block)


def solve_kernel(block, flag_ref, gathered, inverses, rhs, *rest):
    if block:
        first, out, panel_buf, inv_buf, rhs_buf, first_buf, sems = rest
    else:
        out, panel_buf, inv_buf, rhs_buf, sems = rest

    @pl.when(flag_ref[0] == 1)
    def _():
        if block:
            moves = [(first, first_buf), (gathered, panel_buf), (inverses, inv_buf), (rhs, rhs_buf)]
        else:
            moves = [(gathered.at[:, pl.ds(0, NB)], panel_buf), (inverses, inv_buf), (rhs, rhs_buf)]
        copies = [pltpu.make_async_copy(a, b, sems.at[i]) for i, (a, b) in enumerate(moves)]
        for copy in copies:
            copy.start()
        for copy in copies:
            copy.wait()
        base = block * NB
        targets = [rhs_buf[pl.ds(i * Q, Q), :] for i in range(PARTS)]
        if block:
            known = [halves(first_buf[pl.ds(j * Q, Q), :]) for j in range(PARTS)]
            for i in range(PARTS):
                for j in range(PARTS):
                    part = panel_buf[pl.ds(i * Q, Q), pl.ds(j * Q, Q)]
                    targets[i] = targets[i] - product(halves(part), known[j])
        for i in range(PARTS):
            inv = halves(inv_buf[pl.ds(i * Q, Q), :])
            value = product(inv, halves(targets[i]))
            out[pl.ds(i * Q, Q), :] = value
            parts = halves(value)
            for k in range(i + 1, PARTS):
                part = panel_buf[pl.ds(k * Q, Q), pl.ds(base + i * Q, Q)]
                targets[k] = targets[k] - product(halves(part), parts)


def solve(block, flag, gathered, inverses, rhs, *first):
    width = rhs.shape[1]
    buffers = [
        pltpu.VMEM((NB, (1 + block) * NB), F32),
        pltpu.VMEM((NB, Q), F32),
        pltpu.VMEM((NB, width), F32),
    ]
    if block:
        buffers.append(pltpu.VMEM((NB, width), F32))
    return pl.pallas_call(
        functools.partial(solve_kernel, block),
        out_shape=jax.ShapeDtypeStruct((NB, width), F32),
        in_specs=[pl.BlockSpec(memory_space=pltpu.SMEM)] + [pl.BlockSpec(memory_space=pl.ANY)] * (3 + block),
        out_specs=pl.BlockSpec(memory_space=pltpu.VMEM),
        scratch_shapes=buffers + [pltpu.SemaphoreType.DMA((4,))],
        compiler_params=pltpu.CompilerParams(vmem_limit_bytes=48 << 20),
        name="solve%d" % block,
    )(flag, gathered, inverses, rhs, *first)


def split_kernel(value_ref, high_ref, low_ref):
    high, low = halves(value_ref[...])
    high_ref[...] = high
    low_ref[...] = low


def split(value):
    rows, cols = value.shape
    step = 128
    spec = pl.BlockSpec((step, cols), lambda i: (i, 0))
    return pl.pallas_call(
        split_kernel,
        grid=(rows // step,),
        out_shape=[jax.ShapeDtypeStruct(value.shape, BF16)] * 2,
        in_specs=[spec],
        out_specs=[spec, spec],
        compiler_params=pltpu.CompilerParams(vmem_limit_bytes=32 << 20),
        name="split",
    )(value)


def update_kernel(last, place_ref, high_ref, low_ref, target_ref, *rest):
    if last:
        pieces, before, (out, whole, solved_high, solved_low) = rest[:5], rest[5], rest[6:]
    else:
        pieces, (out, whole, solved_high, solved_low) = rest[:5], rest[5:]

    @pl.when(pl.program_id(0) == 0)
    def _():
        if last:
            whole[pl.ds(0, NB), :] = before[...]
        turn = place_ref[0]
        lengths = (Q, Q, Q // 2, Q // 2, Q)
        slots = (0, 1, 2, 2, 3)
        shifts = (0, 0, 0, Q // 2, 0)
        for piece, length, slot, shift in zip(pieces, lengths, slots, shifts):
            start = pl.multiple_of(((slot + turn) & 3) * Q + shift, Q // 2)
            value = piece[...]
            high, low = halves(value)
            solved_high[pl.ds(start, length), :] = high
            solved_low[pl.ds(start, length), :] = low
            whole[pl.ds(start + (NB if last else 0), length), :] = value

    result = target_ref[...] - product((high_ref[...], low_ref[...]), (solved_high[...], solved_low[...]))
    if last:
        out[...] = jnp.where(place_ref[1] >= 2, result, 0.0)
    else:
        out[...] = result


def update(last, place, parts, target, pieces, *before):
    rows, width = target.shape
    step = Q
    panel_spec = pl.BlockSpec((step, NB), lambda i: (i, int(last)))
    target_spec = pl.BlockSpec((step, width), lambda i: (i, 0))

    def fixed(length):
        return pl.BlockSpec((length, width), lambda i: (0, 0))

    held = 2 * NB if last else NB
    return pl.pallas_call(
        functools.partial(update_kernel, last),
        grid=(rows // step,),
        out_shape=[jax.ShapeDtypeStruct((rows, width), F32), jax.ShapeDtypeStruct((held, width), F32)],
        in_specs=[pl.BlockSpec(memory_space=pltpu.SMEM), panel_spec, panel_spec, target_spec]
        + [fixed(piece.shape[0]) for piece in pieces]
        + [fixed(NB)] * len(before),
        out_specs=[target_spec, fixed(held)],
        scratch_shapes=[pltpu.VMEM((NB, width), BF16)] * 2,
        compiler_params=pltpu.CompilerParams(vmem_limit_bytes=48 << 20),
        name="update%d" % int(last),
    )(place, *parts, target, *pieces, *before)


def share_inverses(inverse, row, col):
    y, core = col // 2, col % 2

    def pairs(moves):
        return [(r * COLS + 2 * a + k, r * COLS + 2 * b + k) for r in (0, 1) for a, b in moves[r] for k in (0, 1)]

    both = ("row", "col")
    swap = lax.ppermute(inverse, both, pairs([[(0, 1), (1, 0)], [(2, 3), (3, 2)]]))
    out = lax.ppermute(inverse, both, pairs([[(0, 3), (1, 2)], [(2, 1), (3, 0)]]))
    relay = lax.ppermute(out, both, pairs([[(3, 2), (2, 3)], [(1, 0), (0, 1)]]))
    is_low = y == jnp.where(row == 0, 0, 2)
    is_high = y == jnp.where(row == 0, 1, 3)
    got_low = y == jnp.where(row == 0, 3, 1)
    low = jnp.where(is_low, inverse, jnp.where(is_high, swap, jnp.where(got_low, out, relay)))
    high = jnp.where(is_low, swap, jnp.where(is_high, inverse, jnp.where(got_low, relay, out)))
    mine = jnp.stack([low, high])
    cores = [(r * COLS + c, r * COLS + (c ^ 1)) for r in (0, 1) for c in range(COLS)]
    theirs = lax.ppermute(mine, both, cores)
    first = jnp.where(core == 0, mine, theirs)
    second = jnp.where(core == 0, theirs, mine)
    return jnp.stack([first, second], axis=1).reshape(PARTS * Q, Q)


def spread(solved, root, row, ahead=None):
    z = row // XS

    def piece(i, value=solved):
        return value[i * Q : (i + 1) * Q]

    sent = [i for i in range(1, PARTS) if ahead is None or i != 1]
    mine = jnp.zeros_like(piece(0))
    for i in sent:
        mine = mine + lax.ppermute(piece(i), "row", [(root, (root + i) % XS)])
    if ahead is not None:
        mine = jnp.where(row == root + 1, piece(1, ahead), mine)
    mine = jnp.where(row == root, piece(0), mine)

    def along_z(moves):
        return [(a * XS + x, b * XS + x) for a, b in moves for x in range(XS)]

    near = lax.ppermute(mine, "row", along_z([(0, 3)]))
    far = lax.ppermute(mine, "row", along_z([(0, 5)]))
    mine = jnp.where(z == 0, mine, near + far)
    up = lax.ppermute(mine, "row", along_z([(0, 1), (3, 4), (5, 6)]))
    down = lax.ppermute(mine, "row", along_z([(0, 7), (3, 2)]))
    mine = jnp.where((z == 0) | (z == 3) | (z == 5), mine, up + down)

    to_next = [(r, r // XS * XS + (r + 1) % XS) for r in range(ZS * XS)]
    to_last = [(b, a) for a, b in to_next]
    after = lax.ppermute(mine, "row", to_last)
    before = lax.ppermute(mine, "row", to_next)
    over_top = lax.ppermute(after[: Q // 2], "row", to_last)
    over_rest = lax.ppermute(before[Q // 2 :], "row", to_next)
    return mine, after, over_top, over_rest, before


def body(panel, rhs):
    row = lax.axis_index("row")
    col = lax.axis_index("col")
    gathered = lax.all_gather(panel, "col", axis=1, tiled=True)

    holds = ((row == 0) & (col < PARTS)) | ((row == 1) & (col >= PARTS))
    diagonal = lax.dynamic_slice(panel, ((col % PARTS) * Q, 0), (Q, Q))
    inverse = invert(holds.astype(jnp.int32)[None], diagonal)
    inverses = share_inverses(inverse, row, col)
    parts = split(gathered)

    def flag(r):
        return (row == r).astype(jnp.int32)[None]

    def place(root):
        return jnp.stack([(row - root) % XS, row])

    one = solve(0, flag(0), gathered, inverses, rhs)
    ahead = lax.ppermute(one, "row", [(0, 1)])
    two = solve(1, flag(1), gathered, inverses, rhs, ahead)
    pieces_one = spread(one, 0, row, ahead)
    pieces_two = spread(two, 1, row)
    updated, solved_one = update(False, place(0), parts, rhs, pieces_one)
    return tuple(update(True, place(1), parts, updated, pieces_two, solved_one))


def solution(mesh):
    placed = (P("row", "col"), P("row", "col"))
    return jax.shard_map(
        body,
        mesh=mesh,
        in_specs=placed,
        out_specs=(P("row", "col"), P(None, "col")),
        check_vma=False,
    )
```

```python
import functools

import jax
import jax.numpy as jnp
from jax import lax
from jax.experimental import pallas as pl
from jax.experimental.pallas import tpu as pltpu
from jax.sharding import PartitionSpec as P

NB = 1024
HALF = NB // 2
Q = 256
PARTS = 4
XS = 4
YS = 4
ZS = 8
ROWS = XS * ZS
COLS = 2 * YS
F32 = jnp.float32
BF16 = jnp.bfloat16
BOTH = ("row", "col")


def halves(value):
    high = value.astype(BF16)
    return high, (value - high.astype(F32)).astype(BF16)


def product(left, right):
    dot = functools.partial(jnp.dot, preferred_element_type=F32)
    return dot(left[0], right[0]) + (dot(left[0], right[1]) + dot(left[1], right[0]))


def call(kernel, name, shapes, scratch, operands, in_specs=None, out_specs=None, vmem=24, **options):
    operands = [pltpu.with_memory_space_constraint(x, pltpu.HBM) if x.ndim == 3 else x for x in operands]
    return pl.pallas_call(
        kernel,
        out_shape=[(pltpu.HBM if len(shape) == 3 else jax.ShapeDtypeStruct)(shape, dtype) for shape, dtype in shapes],
        in_specs=[pl.BlockSpec(memory_space=pltpu.SMEM)]
        + (in_specs or [pl.BlockSpec(memory_space=pl.ANY)] * (len(operands) - 1)),
        out_specs=out_specs or [pl.BlockSpec(memory_space=pltpu.VMEM)] * len(shapes),
        scratch_shapes=scratch,
        compiler_params=pltpu.CompilerParams(vmem_limit_bytes=vmem << 20),
        cost_estimate=pl.CostEstimate(flops=2 * NB * NB * Q, bytes_accessed=8 << 20, transcendentals=0),
        name=name,
        **options,
    )(*operands)


ROW, PLACE_Y, CORE, TURN = range(4)


def payload_kernel(place, panel_ref, top_ref, bottom_ref):
    top_ref[...] = panel_ref[pl.ds(0, HALF), :]
    bottom_ref[...] = panel_ref[pl.ds(HALF, HALF), :]
    col = 2 * place[PLACE_Y] + place[CORE]
    number = col & (PARTS - 1)

    @pl.when(((place[ROW] == 0) & (col < PARTS)) | ((place[ROW] == 1) & (col >= PARTS)))
    def _():
        rows = lax.broadcasted_iota(jnp.int32, (Q, Q), 0)
        cols = lax.broadcasted_iota(jnp.int32, (Q, Q), 1)
        block = panel_ref[pl.ds(pl.multiple_of(number * Q, Q), Q), :]
        inverse = jnp.where(rows == cols, 1.0 / jnp.where(rows == cols, block, 1.0), 0.0)
        level = 0
        while (1 << level) < Q:
            pair = (rows >> (level + 1)) == (cols >> (level + 1))
            below = pair & (((rows >> level) & 1) == 1) & (((cols >> level) & 1) == 0)
            parts = halves(inverse)
            inner = product(halves(jnp.where(below, block, 0.0)), parts)
            inverse = inverse - product(parts, halves(inner))
            level += 1
        for i in range(PARTS):

            @pl.when(number == i)
            def _():
                half = (top_ref, bottom_ref)[i // 2]
                half[pl.ds((i % 2) * Q, Q), :] = inverse


def payload(place, panel):
    vmem = [pl.BlockSpec(memory_space=pltpu.VMEM)]
    return call(payload_kernel, "payload", [((HALF, Q), F32)] * 2, [], (place, panel), in_specs=vmem)


CHUNK = tuple(
    (step, same, start, length)
    for step, start, length in ((0, 0, HALF), (1, 0, HALF), (3, 0, HALF), (2, 0, Q), (2, Q, Q))
    for same in (True, False)
)


def pairs(step, origin, has):
    return [
        (r * COLS + 2 * y + k, r * COLS + 2 * ((y + step) % YS) + k)
        for r in range(ROWS)
        for y in range(YS)
        for k in (0, 1)
        if has(r, (y + origin) % YS)
    ]


def other_core(value):
    return lax.ppermute(value, "col", [(c, c ^ 1) for c in range(COLS)])


def near_chips(chunk, has):
    behind = lax.ppermute(chunk, BOTH, pairs(1, 0, has))
    return lax.ppermute(chunk, BOTH, pairs(-1, 0, has)), behind


def far_chip(ahead, behind, has):
    return lax.ppermute(ahead[:Q], BOTH, pairs(-1, 1, has)), lax.ppermute(behind[Q:], BOTH, pairs(1, -1, has))


def both_cores(values):
    return [x for value in values for x in (value, other_core(value))]


def collect(place, arrays, blocks, buffer, first, sem):
    for (step, same, start, length), array in zip(CHUNK, arrays):
        core = place[CORE] if same else 1 - place[CORE]
        block = 2 * ((place[PLACE_Y] + step) & (YS - 1)) + core

        @pl.when(block < blocks)
        def _():
            pltpu.make_async_copy(array, buffer.at[block, pl.ds(first + start, length)], sem).start()


def assemble_kernel(place, *rest):
    arrays, (out, sem) = rest[: len(CHUNK)], rest[len(CHUNK) :]
    collect(place, arrays, COLS, out, 0, sem)
    pltpu.make_async_copy(out, out, sem).wait()


def assemble(place, arrays):
    in_hbm = [pl.BlockSpec(memory_space=pltpu.HBM)]
    scratch = [pltpu.SemaphoreType.DMA]
    shapes = [((COLS, HALF, Q), F32)]
    return call(assemble_kernel, "assemble", shapes, scratch, (place, *arrays), out_specs=in_hbm)[0]


def blocks_copies(top, bottom, base, buffer, sems):
    copies = [
        pltpu.make_async_copy(half.at[pl.ds(base, PARTS)], buffer.at[:, pl.ds(i * HALF, HALF)], sems.at[i])
        for i, half in enumerate((top, bottom))
    ]
    for copy in copies:
        copy.start()
    return copies


def eliminate(triangle, targets, store):
    for i in range(PARTS):
        value = product(halves(triangle[i, pl.ds(i * Q, Q), :]), halves(targets[i]))
        store(i, value)
        parts = halves(value)
        for k in range(i + 1, PARTS):
            targets[k] = targets[k] - product(halves(triangle[i, pl.ds(k * Q, Q), :]), parts)


def solve_kernel(place, rhs, top, *rest):
    bottoms, rest = rest[: len(CHUNK)], rest[len(CHUNK) :]
    one, two, three, others, triangle, rhs_buf, sem, top_sem, rhs_sem = rest

    @pl.when(place[ROW] == 0)
    def _():
        lower = triangle.at[:, pl.ds(HALF, HALF)]
        collect(place, bottoms, PARTS, triangle, HALF, sem)
        copies = [
            pltpu.make_async_copy(rhs, rhs_buf, rhs_sem),
            pltpu.make_async_copy(top.at[pl.ds(0, PARTS)], triangle.at[:, pl.ds(0, HALF)], top_sem),
        ]
        for copy in copies:
            copy.start()
        for copy in copies:
            copy.wait()
        pltpu.make_async_copy(lower, lower, sem).wait()

        def store(i, value):
            if i == 1:
                one[...] = value
            else:
                others[pl.ds(max(i - 1, 0) * Q, Q), :] = value
            if i >= 2:
                (two, three)[i - 2][...] = value

        eliminate(triangle, [rhs_buf[pl.ds(i * Q, Q), :] for i in range(PARTS)], store)


def solve(place, rhs, top, bottoms):
    scratch = [
        pltpu.VMEM((PARTS, NB, Q), F32),
        pltpu.VMEM((NB, Q), F32),
        pltpu.SemaphoreType.DMA,
        pltpu.SemaphoreType.DMA,
        pltpu.SemaphoreType.DMA,
    ]
    shapes = [((Q, Q), F32)] * 3 + [((3 * Q, Q), F32)]
    return call(solve_kernel, "solve", shapes, scratch, (place, rhs, top, *bottoms))


def second_kernel(place, rhs, top, bottom, one, others, *rest):
    out, (triangle, left, rhs_buf, first_buf, sem, left_sem, rhs_sem, first_sem) = rest[:PARTS], rest[PARTS:]

    @pl.when(place[ROW] == 1)
    def _():
        copies = [pltpu.make_async_copy(rhs, rhs_buf, rhs_sem)]
        for i, (array, start, at, length) in enumerate(((others, 0, 0, Q), (one, 0, Q, Q), (others, Q, 2 * Q, 2 * Q))):
            source = array.at[pl.ds(start, length)]
            copies.append(pltpu.make_async_copy(source, first_buf.at[pl.ds(at, length)], first_sem.at[i]))
        for copy in copies:
            copy.start()
        copies += blocks_copies(top, bottom, 0, left, left_sem)
        later = blocks_copies(top, bottom, PARTS, triangle, sem)
        for copy in copies:
            copy.wait()
        solved = [halves(first_buf[pl.ds(j * Q, Q), :]) for j in range(PARTS)]
        targets = []
        for i in range(PARTS):
            rows = pl.ds(i * Q, Q)
            value = rhs_buf[rows, :]
            for j in range(PARTS):
                value = value - product(halves(left[j, rows, :]), solved[j])
            targets.append(value)
        for copy in later:
            copy.wait()

        def store(i, value):
            out[i][...] = value

        eliminate(triangle, targets, store)


def second(place, rhs, top, bottom, one, others):
    scratch = [
        pltpu.VMEM((PARTS, NB, Q), F32),
        pltpu.VMEM((PARTS, NB, Q), F32),
        pltpu.VMEM((NB, Q), F32),
        pltpu.VMEM((NB, Q), F32),
        pltpu.SemaphoreType.DMA((2,)),
        pltpu.SemaphoreType.DMA((2,)),
        pltpu.SemaphoreType.DMA,
        pltpu.SemaphoreType.DMA((3,)),
    ]
    return call(second_kernel, "second", [((Q, Q), F32)] * PARTS, scratch, (place, rhs, top, bottom, one, others))


PIECES = ((0, Q), (Q, Q), (2 * Q, Q // 2), (2 * Q + Q // 2, Q // 2), (3 * Q, Q))


def update_kernel(last, place, target, top, bottom, *rest):
    pieces, rest = rest[: len(PIECES)], rest[len(PIECES) + int(last) :]
    out, whole, blocks, target_buf, solved_buf, panel_high, panel_low, sem, target_sem, solved_sem, whole_sem = rest
    base = PARTS * int(last)
    for piece, (at, length) in zip(pieces, PIECES):
        start = pl.multiple_of((at + place[TURN] * Q) & (NB - 1), Q // 2)
        pltpu.make_async_copy(piece, solved_buf.at[pl.ds(start, length)], solved_sem).start()
    waits = blocks_copies(top, bottom, base, blocks, sem)
    copy = pltpu.make_async_copy(target, target_buf, target_sem)
    copy.start()
    pltpu.make_async_copy(solved_buf, solved_buf, solved_sem).wait()
    keep = pltpu.make_async_copy(solved_buf, whole.at[pl.ds(int(last) * NB, NB)], whole_sem)
    keep.start()
    solved = halves(solved_buf[...])
    for wait in waits:
        wait.wait()
    for j in range(PARTS):
        high, low = halves(blocks[j])
        panel_high[:, j * Q : (j + 1) * Q] = high
        panel_low[:, j * Q : (j + 1) * Q] = low
    copy.wait()
    for i in range(PARTS):
        rows = pl.ds(i * Q, Q)
        result = target_buf[rows, :] - product((panel_high[rows, :], panel_low[rows, :]), solved)
        out[rows, :] = jnp.where(place[ROW] >= 2, result, 0.0) if last else result
    keep.wait()


def update(last, place, target, top, bottom, pieces, *before):
    scratch = [
        pltpu.VMEM((PARTS, NB, Q), F32),
        pltpu.VMEM((NB, Q), F32),
        pltpu.VMEM((NB, Q), F32),
        pltpu.VMEM((NB, NB), BF16),
        pltpu.VMEM((NB, NB), BF16),
        pltpu.SemaphoreType.DMA((2,)),
        pltpu.SemaphoreType.DMA,
        pltpu.SemaphoreType.DMA,
        pltpu.SemaphoreType.DMA,
    ]
    operands = (place, target, top, bottom, *pieces, *before)
    return call(
        functools.partial(update_kernel, last),
        "update%d" % int(last),
        [((NB, Q), F32), ((2 * NB, Q), F32)],
        scratch,
        operands,
        out_specs=[pl.BlockSpec(memory_space=pltpu.VMEM), pl.BlockSpec(memory_space=pl.ANY)],
        input_output_aliases={len(operands) - 1: 1} if before else {},
    )


def along_z(moves):
    return [(a * XS + x, b * XS + x) for a, b in moves for x in range(XS)]


TO_NEXT = [(r, r // XS * XS + (r + 1) % XS) for r in range(ROWS)]
TO_LAST = [(b, a) for a, b in TO_NEXT]


def scatter(pieces, root):
    got = [lax.ppermute(pieces[i], "row", [(root, (root + i) % XS)]) for i in (2, 1, 3)]
    return got[1], got[0], got[2]


def far_z(mine, z):
    near = lax.ppermute(mine, "row", along_z([(0, 3)]))
    far = lax.ppermute(mine, "row", along_z([(0, 5)]))
    return jnp.where(z == 0, mine, near + far)


def near_z(mine, z):
    up = lax.ppermute(mine, "row", along_z([(0, 1), (3, 4), (5, 6)]))
    down = lax.ppermute(mine, "row", along_z([(0, 7), (3, 2)]))
    return jnp.where((z == 0) | (z == 3) | (z == 5), mine, up + down)


def over_x(mine):
    after = lax.ppermute(mine, "row", TO_LAST)
    before = lax.ppermute(mine, "row", TO_NEXT)
    over_top = lax.ppermute(after[: Q // 2], "row", TO_LAST)
    over_rest = lax.ppermute(before[Q // 2 :], "row", TO_NEXT)
    return mine, after, over_top, over_rest, before


def body(panel, rhs):
    row = lax.axis_index("row")
    col = lax.axis_index("col")
    z = row // XS

    def place(root):
        return jnp.stack([row, col // 2, col % 2, (row - root) % XS])

    def after(value, *others):
        return lax.optimization_barrier((value, *others))[0]

    top, bottom = payload(place(0), panel)
    near = near_chips(top, lambda r, y: r > 0 or y == 0)
    top = assemble(place(0), both_cores((top, *near, *far_chip(*near, lambda r, y: r > 0 or y == 0))))
    near = near_chips(bottom, lambda r, y: r > 0 or y <= 1)
    bottoms = both_cores((bottom, *near, *far_chip(*near, lambda r, y: r > 0 or y <= 1)))
    one, two, three, others = solve(place(0), rhs, top, bottoms)
    others_ahead = lax.ppermute(others, "row", [(0, 1)])
    one_ahead, two_ahead, three_ahead = scatter((None, one, two, three), 0)
    bottom = assemble(place(0), bottoms)
    mine_one = jnp.where(row == 0, others[:Q], one_ahead + two_ahead + three_ahead)
    mine_one = far_z(mine_one, z)

    pieces = second(place(0), rhs, top, bottom, one_ahead, others_ahead)
    got = scatter(pieces, 1)
    mine_one = near_z(after(mine_one, *pieces), z)
    mine_two = jnp.where(row == 1, pieces[0], got[0] + got[1] + got[2])
    pieces_one = over_x(after(mine_one, mine_two))
    mine_two = far_z(mine_two, z)
    updated, whole = update(False, place(0), rhs, top, bottom, pieces_one)
    mine_two, updated, whole = lax.optimization_barrier((mine_two, updated, whole))
    pieces_two = over_x(near_z(mine_two, z))
    return tuple(update(True, place(1), updated, top, bottom, pieces_two, whole))


def solution(mesh):
    placed = (P("row", "col"), P("row", "col"))
    return jax.shard_map(
        body,
        mesh=mesh,
        in_specs=placed,
        out_specs=(P("row", "col"), P(None, "col")),
        check_vma=False,
    )
```

```python
import functools

import jax
import jax.numpy as jnp
from jax import lax
from jax.experimental import pallas as pl
from jax.experimental.pallas import tpu as pltpu
from jax.sharding import PartitionSpec as P

NB = 1024
HALF = NB // 2
Q = 256
PARTS = 4
XS = 4
YS = 4
ZS = 8
ROWS = XS * ZS
COLS = 2 * YS
F32 = jnp.float32
BF16 = jnp.bfloat16
BOTH = ("row", "col")
UPDATE_COST = 60


def halves(value):
    high = value.astype(BF16)
    return high, (value - high.astype(F32)).astype(BF16)


def product(left, right):
    dot = functools.partial(jnp.dot, preferred_element_type=F32)
    return dot(left[0], right[0]) + (dot(left[0], right[1]) + dot(left[1], right[0]))


def call(kernel, name, shapes, scratch, operands, in_specs=None, out_specs=None, vmem=24, flops=2 * NB * NB * Q, **options):
    operands = [pltpu.with_memory_space_constraint(x, pltpu.HBM) if x.ndim == 3 else x for x in operands]
    return pl.pallas_call(
        kernel,
        out_shape=[(pltpu.HBM if len(shape) == 3 else jax.ShapeDtypeStruct)(shape, dtype) for shape, dtype in shapes],
        in_specs=[pl.BlockSpec(memory_space=pltpu.SMEM)]
        + (in_specs or [pl.BlockSpec(memory_space=pl.ANY)] * (len(operands) - 1)),
        out_specs=out_specs or [pl.BlockSpec(memory_space=pltpu.VMEM)] * len(shapes),
        scratch_shapes=scratch,
        compiler_params=pltpu.CompilerParams(vmem_limit_bytes=vmem << 20),
        cost_estimate=pl.CostEstimate(flops=flops, bytes_accessed=8 << 20, transcendentals=0),
        name=name,
        **options,
    )(*operands)


ROW, PLACE_Y, CORE, TURN = range(4)


def payload_kernel(place, panel_ref, top_ref, bottom_ref):
    top_ref[...] = panel_ref[pl.ds(0, HALF), :]
    bottom_ref[...] = panel_ref[pl.ds(HALF, HALF), :]
    col = 2 * place[PLACE_Y] + place[CORE]
    number = col & (PARTS - 1)

    @pl.when(((place[ROW] == 0) & (col < PARTS)) | ((place[ROW] == 1) & (col >= PARTS)))
    def _():
        rows = lax.broadcasted_iota(jnp.int32, (Q, Q), 0)
        cols = lax.broadcasted_iota(jnp.int32, (Q, Q), 1)
        block = panel_ref[pl.ds(pl.multiple_of(number * Q, Q), Q), :]
        inverse = jnp.where(rows == cols, 1.0 / jnp.where(rows == cols, block, 1.0), 0.0)
        level = 0
        while (1 << level) < Q:
            pair = (rows >> (level + 1)) == (cols >> (level + 1))
            below = pair & (((rows >> level) & 1) == 1) & (((cols >> level) & 1) == 0)
            parts = halves(inverse)
            inner = product(halves(jnp.where(below, block, 0.0)), parts)
            inverse = inverse - product(parts, halves(inner))
            level += 1
        for i in range(PARTS):

            @pl.when(number == i)
            def _():
                half = (top_ref, bottom_ref)[i // 2]
                half[pl.ds((i % 2) * Q, Q), :] = inverse


def payload(place, panel):
    vmem = [pl.BlockSpec(memory_space=pltpu.VMEM)]
    return call(payload_kernel, "payload", [((HALF, Q), F32)] * 2, [], (place, panel), in_specs=vmem)


CHUNK = tuple((step, same) for step in (0, 1, 3, 2) for same in (True, False))


def pairs(step, origin, has):
    return [
        (r * COLS + 2 * y + k, r * COLS + 2 * ((y + step) % YS) + k)
        for r in range(ROWS)
        for y in range(YS)
        for k in (0, 1)
        if has(r, (y + origin) % YS)
    ]


def other_core(value):
    return lax.ppermute(value, "col", [(c, c ^ 1) for c in range(COLS)])


def near_chips(chunk, has):
    behind = lax.ppermute(chunk, BOTH, pairs(1, 0, has))
    return lax.ppermute(chunk, BOTH, pairs(-1, 0, has)), behind


def far_chip(ahead, behind, has):
    if behind is None:
        return lax.ppermute(ahead, BOTH, pairs(-1, 1, has))
    return lax.ppermute(behind, BOTH, pairs(1, -1, has))


def both_cores(values):
    return [x for value in values for x in (value, other_core(value))]


def assemble_kernel(place, *rest):
    arrays, (out, sem) = rest[: len(CHUNK)], rest[len(CHUNK) :]
    blocks = jnp.where(place[ROW] == 0, PARTS, COLS)
    for wait in (False, True):
        for (step, same), array in zip(CHUNK, arrays):
            core = place[CORE] if same else 1 - place[CORE]
            block = 2 * ((place[PLACE_Y] + step) & (YS - 1)) + core

            @pl.when(block < blocks)
            def _():
                copy = pltpu.make_async_copy(array, out.at[block], sem.at[block])
                copy.wait() if wait else copy.start()


def assemble(place, arrays):
    in_hbm = [pl.BlockSpec(memory_space=pltpu.HBM)]
    scratch = [pltpu.SemaphoreType.DMA((COLS,))]
    shapes = [((COLS, HALF, Q), F32)]
    return call(assemble_kernel, "assemble", shapes, scratch, (place, *arrays), out_specs=in_hbm)[0]


def blocks_copies(top, bottom, base, buffer, sems):
    copies = [
        pltpu.make_async_copy(half.at[pl.ds(base, PARTS)], buffer.at[:, pl.ds(i * HALF, HALF)], sems.at[i])
        for i, half in enumerate((top, bottom))
    ]
    for copy in copies:
        copy.start()
    return copies


def eliminate(triangle, targets, store):
    for i in range(PARTS):
        value = product(halves(triangle[i, pl.ds(i * Q, Q), :]), halves(targets[i]))
        store(i, value)
        parts = halves(value)
        for k in range(i + 1, PARTS):
            targets[k] = targets[k] - product(halves(triangle[i, pl.ds(k * Q, Q), :]), parts)


def solve_kernel(place, rhs, top, bottom, whole, two, three, triangle, rhs_buf, sem, rhs_sem):
    @pl.when(place[ROW] == 0)
    def _():
        copy = pltpu.make_async_copy(rhs, rhs_buf, rhs_sem)
        copy.start()
        for wait in blocks_copies(top, bottom, 0, triangle, sem):
            wait.wait()
        copy.wait()

        def store(i, value):
            whole[pl.ds(i * Q, Q), :] = value
            if i >= 2:
                (two, three)[i - 2][...] = value

        eliminate(triangle, [rhs_buf[pl.ds(i * Q, Q), :] for i in range(PARTS)], store)


def solve(place, rhs, top, bottom):
    scratch = [
        pltpu.VMEM((PARTS, NB, Q), F32),
        pltpu.VMEM((NB, Q), F32),
        pltpu.SemaphoreType.DMA((2,)),
        pltpu.SemaphoreType.DMA,
    ]
    shapes = [((NB, Q), F32), ((Q, Q), F32), ((Q, Q), F32)]
    return call(solve_kernel, "solve", shapes, scratch, (place, rhs, top, bottom))


def prepare_kernel(place, rhs, top, bottom, w_high, w_low, y_out, triangle, targets, sem, left_sem, rhs_sem):
    @pl.when(place[ROW] == 1)
    def _():
        copies = [pltpu.make_async_copy(rhs, targets.at[:, pl.ds(NB, Q)], rhs_sem)]
        for j in range(PARTS):
            for i, half in enumerate((top, bottom)):
                target = targets.at[pl.ds(i * HALF, HALF), pl.ds(j * Q, Q)]
                copies.append(pltpu.make_async_copy(half.at[j], target, left_sem.at[2 * j + i]))
        for copy in copies:
            copy.start()
        for copy in (*blocks_copies(top, bottom, PARTS, triangle, sem), *copies):
            copy.wait()
        for i in range(PARTS):
            rows = pl.ds(i * Q, Q)
            value = product(halves(triangle[i, rows, :]), halves(targets[rows, :]))
            parts = halves(value)
            w_high[rows, :], w_low[rows, :] = parts[0][:, :NB], parts[1][:, :NB]
            y_out[rows, :] = value[:, NB:]
            for k in range(i + 1, PARTS):
                below = pl.ds(k * Q, Q)
                targets[below, :] -= product(halves(triangle[i, below, :]), parts)


def prepare(place, rhs, top, bottom):
    scratch = [
        pltpu.VMEM((PARTS, NB, Q), F32),
        pltpu.VMEM((NB, NB + Q), F32),
        pltpu.SemaphoreType.DMA((2,)),
        pltpu.SemaphoreType.DMA((2 * PARTS,)),
        pltpu.SemaphoreType.DMA,
    ]
    shapes = [((NB, NB), BF16)] * 2 + [((NB, Q), F32)]
    return call(prepare_kernel, "prepare", shapes, scratch, (place, rhs, top, bottom), vmem=32)


def combine_kernel(place, w_high, w_low, y_ref, first, *out):
    @pl.when(place[ROW] == 1)
    def _():
        solved = halves(first[...])
        for i in range(PARTS):
            rows = pl.ds(i * Q, Q)
            out[i][...] = y_ref[rows, :] - product((w_high[rows, :], w_low[rows, :]), solved)


def combine(place, w_high, w_low, y_value, first):
    vmem = [pl.BlockSpec(memory_space=pltpu.VMEM)] * 4
    operands = (place, w_high, w_low, y_value, first)
    return call(combine_kernel, "combine", [((Q, Q), F32)] * PARTS, [], operands, in_specs=vmem)


PIECES = ((0, Q), (Q, Q), (2 * Q, Q // 2), (2 * Q + Q // 2, Q // 2), (3 * Q, Q))


def update_kernel(base, slots, last, place, target, top, bottom, *rest):
    used = [n for n, (at, _) in enumerate(PIECES) if at // Q in slots]
    pieces, rest = rest[: len(used)], rest[len(used) + int(base + len(slots) > PARTS) :]
    out, whole, blocks, target_buf, solved_buf, sem, target_sem, solved_sem, whole_sem = rest
    copies, kept = [], []
    for i, (n, piece) in enumerate(zip(used, pieces)):
        at, length = PIECES[n]
        here = pl.ds(slots.index(at // Q) * Q + at % Q, length)
        copies.append(pltpu.make_async_copy(piece, solved_buf.at[here], solved_sem.at[i]))
        start = pl.multiple_of(((at + place[TURN] * Q) & (NB - 1)) + base * Q, Q // 2)
        kept.append(pltpu.make_async_copy(solved_buf.at[here], whole.at[pl.ds(start, length)], whole_sem.at[i]))
    copies.append(pltpu.make_async_copy(target, target_buf, target_sem))
    for i, slot in enumerate(slots):
        block = base + ((slot + place[TURN]) & (PARTS - 1))
        for k, half in enumerate((top, bottom)):
            copies.append(
                pltpu.make_async_copy(half.at[block], blocks.at[i, pl.ds(k * HALF, HALF)], sem.at[2 * i + k])
            )
    for copy in copies:
        copy.start()
    for copy in copies[: len(used)]:
        copy.wait()
    for copy in kept:
        copy.start()
    solved = [halves(solved_buf[pl.ds(i * Q, Q), :]) for i in range(len(slots))]
    for copy in copies[len(used) :]:
        copy.wait()
    for r in range(PARTS):
        rows = pl.ds(r * Q, Q)
        result = target_buf[rows, :]
        for i in range(len(slots)):
            result = result - product(halves(blocks[i, rows, :]), solved[i])
        out[rows, :] = jnp.where(place[ROW] >= 2, result, 0.0) if last else result
    for copy in kept:
        copy.wait()


def update(name, base, slots, last, place, target, top, bottom, pieces, *before):
    scratch = [
        pltpu.VMEM((len(slots), NB, Q), F32),
        pltpu.VMEM((NB, Q), F32),
        pltpu.VMEM((len(slots) * Q, Q), F32),
        pltpu.SemaphoreType.DMA((2 * len(slots),)),
        pltpu.SemaphoreType.DMA,
        pltpu.SemaphoreType.DMA((len(pieces),)),
        pltpu.SemaphoreType.DMA((len(pieces),)),
    ]
    operands = (place, target, top, bottom, *pieces, *before)
    return call(
        functools.partial(update_kernel, base, slots, last),
        name,
        [((NB, Q), F32), ((2 * NB, Q), F32)],
        scratch,
        operands,
        out_specs=[pl.BlockSpec(memory_space=pltpu.VMEM), pl.BlockSpec(memory_space=pl.ANY)],
        input_output_aliases={len(operands) - 1: 1} if before else {},
        flops=(6 if before else UPDATE_COST) * NB * NB * Q,
    )


def along_z(moves):
    return [(a * XS + x, b * XS + x) for a, b in moves for x in range(XS)]


TO_NEXT = [(r, r // XS * XS + (r + 1) % XS) for r in range(ROWS)]
TO_LAST = [(b, a) for a, b in TO_NEXT]


def after(value, *others):
    return lax.optimization_barrier((value, *others))[0]


def scatter_first(two, three):
    relay = lax.ppermute(two, "row", [(0, 3)])
    return lax.ppermute(relay, "row", [(3, 2)]), lax.ppermute(three, "row", [(0, 3)])


def scatter_second(pieces):
    return [lax.ppermute(pieces[i], "row", [(1, (1 + i) % XS)]) for i in (1, 2, 3)]


def far_z(mine, z):
    near = lax.ppermute(mine, "row", along_z([(0, 3)]))
    far = lax.ppermute(mine, "row", along_z([(0, 5)]))
    return jnp.where(z == 0, mine, near + far)


def near_z(mine, z):
    up = lax.ppermute(mine, "row", along_z([(0, 1), (3, 4), (5, 6)]))
    down = lax.ppermute(mine, "row", along_z([(0, 7), (3, 2)]))
    return jnp.where((z == 0) | (z == 3) | (z == 5), mine, up + down)


def over_x(mine):
    return lax.ppermute(mine, "row", TO_LAST), lax.ppermute(mine, "row", TO_NEXT)


def across_x(after, before):
    return lax.ppermute(after[: Q // 2], "row", TO_LAST), lax.ppermute(before[Q // 2 :], "row", TO_NEXT)


def body(panel, rhs):
    row = lax.axis_index("row")
    col = lax.axis_index("col")
    z = row // XS

    def place(root):
        return jnp.stack([row, col // 2, col % 2, (row - root) % XS])

    def after(value, *others):
        return lax.optimization_barrier((value, *others))[0]

    top, bottom = payload(place(0), panel)
    top_near = near_chips(top, lambda r, y: r > 0 or y == 0)
    bottom_near = near_chips(bottom, lambda r, y: r > 0 or y <= 1)
    top_far = far_chip(top_near[0], None, lambda r, y: r > 0 or y == 0)
    bottom_far = far_chip(None, bottom_near[1], lambda r, y: r > 0 or y <= 1)
    top = assemble(place(0), both_cores((top, *top_near, top_far)))
    bottom = assemble(place(0), both_cores((bottom, *bottom_near, bottom_far)))

    first, two, three = solve(place(0), rhs, top, bottom)
    ahead = lax.ppermute(first, "row", [(0, 1)])
    two_ahead, three_ahead = scatter_first(two, three)
    w_high, w_low, y_value = prepare(place(0), rhs, top, bottom)
    mine_one = jnp.where(row == 1, ahead[Q : 2 * Q], two_ahead + three_ahead)
    mine_one = far_z(after(jnp.where(row == 0, first[:Q], mine_one), w_high), z)

    pieces = combine(place(0), w_high, w_low, y_value, ahead)
    got = scatter_second(pieces)
    mine_one = near_z(after(mine_one, *pieces), z)
    mine_two = jnp.where(row == 1, pieces[0], got[0] + got[1] + got[2])
    beside_one = over_x(after(mine_one, got[0]))
    across_one = across_x(*beside_one)
    mine_two = far_z(mine_two, z)
    pieces_one = [after(x, mine_two) for x in (mine_one, beside_one[0], *across_one, beside_one[1])]
    updated, whole = update("update", 0, (0, 1, 2, 3), False, place(0), rhs, top, bottom, pieces_one)
    mine_two = near_z(mine_two, z)
    beside_two = [after(piece, updated) for piece in over_x(mine_two)]
    across_two = across_x(*beside_two)
    pieces_two = (mine_two, *beside_two)
    updated, whole = update("most", PARTS, (0, 1, 3), False, place(1), updated, top, bottom, pieces_two, whole)
    return tuple(update("last", PARTS, (2,), True, place(1), updated, top, bottom, across_two, whole))


def solution(mesh):
    placed = (P("row", "col"), P("row", "col"))
    return jax.shard_map(
        body,
        mesh=mesh,
        in_specs=placed,
        out_specs=(P("row", "col"), P(None, "col")),
        check_vma=False,
    )
```

```python
import functools

import jax
import jax.numpy as jnp
from jax import lax
from jax.experimental import pallas as pl
from jax.experimental.pallas import tpu as pltpu
from jax.sharding import PartitionSpec as P

NB = 1024
HALF = NB // 2
Q = 256
PARTS = 4
XS = 4
YS = 4
ZS = 8
ROWS = XS * ZS
COLS = 2 * YS
F32 = jnp.float32
BF16 = jnp.bfloat16
BOTH = ("row", "col")
UPDATE_COST = 60


def halves(value):
    high = value.astype(BF16)
    return high, (value - high.astype(F32)).astype(BF16)


def product(left, right):
    dot = functools.partial(jnp.dot, preferred_element_type=F32)
    return dot(left[0], right[0]) + (dot(left[0], right[1]) + dot(left[1], right[0]))


def call(kernel, name, shapes, scratch, operands, in_specs=None, out_specs=None, vmem=24, flops=2 * NB * NB * Q, **options):
    operands = [pltpu.with_memory_space_constraint(x, pltpu.HBM) if x.ndim == 3 else x for x in operands]
    return pl.pallas_call(
        kernel,
        out_shape=[(pltpu.HBM if len(shape) == 3 else jax.ShapeDtypeStruct)(shape, dtype) for shape, dtype in shapes],
        in_specs=[pl.BlockSpec(memory_space=pltpu.SMEM)]
        + (in_specs or [pl.BlockSpec(memory_space=pl.ANY)] * (len(operands) - 1)),
        out_specs=out_specs or [pl.BlockSpec(memory_space=pltpu.VMEM)] * len(shapes),
        scratch_shapes=scratch,
        compiler_params=pltpu.CompilerParams(vmem_limit_bytes=vmem << 20),
        cost_estimate=pl.CostEstimate(flops=flops, bytes_accessed=8 << 20, transcendentals=0),
        name=name,
        **options,
    )(*operands)


ROW, PLACE_Y, CORE, TURN = range(4)


def payload_kernel(place, panel_ref, top_ref, bottom_ref):
    top_ref[...] = panel_ref[pl.ds(0, HALF), :]
    bottom_ref[...] = panel_ref[pl.ds(HALF, HALF), :]
    col = 2 * place[PLACE_Y] + place[CORE]
    number = col & (PARTS - 1)

    @pl.when(((place[ROW] == 0) & (col < PARTS)) | ((place[ROW] == 1) & (col >= PARTS)))
    def _():
        rows = lax.broadcasted_iota(jnp.int32, (Q, Q), 0)
        cols = lax.broadcasted_iota(jnp.int32, (Q, Q), 1)
        block = panel_ref[pl.ds(pl.multiple_of(number * Q, Q), Q), :]
        inverse = jnp.where(rows == cols, 1.0 / jnp.where(rows == cols, block, 1.0), 0.0)
        level = 0
        while (1 << level) < Q:
            pair = (rows >> (level + 1)) == (cols >> (level + 1))
            below = pair & (((rows >> level) & 1) == 1) & (((cols >> level) & 1) == 0)
            parts = halves(inverse)
            inner = product(halves(jnp.where(below, block, 0.0)), parts)
            inverse = inverse - product(parts, halves(inner))
            level += 1
        for i in range(PARTS):

            @pl.when(number == i)
            def _():
                half = (top_ref, bottom_ref)[i // 2]
                half[pl.ds((i % 2) * Q, Q), :] = inverse


def payload(place, panel):
    vmem = [pl.BlockSpec(memory_space=pltpu.VMEM)]
    return call(payload_kernel, "payload", [((HALF, Q), F32)] * 2, [], (place, panel), in_specs=vmem)


CHUNK = tuple((step, same) for step in (0, 1, 3, 2) for same in (True, False))


def pairs(step, origin, has):
    return [
        (r * COLS + 2 * y + k, r * COLS + 2 * ((y + step) % YS) + k)
        for r in range(ROWS)
        for y in range(YS)
        for k in (0, 1)
        if has(r, (y + origin) % YS)
    ]


def other_core(value):
    return lax.ppermute(value, "col", [(c, c ^ 1) for c in range(COLS)])


def near_chips(chunk, has):
    behind = lax.ppermute(chunk, BOTH, pairs(1, 0, has))
    return lax.ppermute(chunk, BOTH, pairs(-1, 0, has)), behind


def far_chip(ahead, behind, has):
    if behind is None:
        return lax.ppermute(ahead, BOTH, pairs(-1, 1, has))
    return lax.ppermute(behind, BOTH, pairs(1, -1, has))


def both_cores(values):
    return [x for value in values for x in (value, other_core(value))]


def place_blocks(place, arrays, chosen, out, sem):
    def each(act):
        for n, ((step, same), array) in enumerate(zip(CHUNK, arrays)):
            core = place[CORE] if same else 1 - place[CORE]
            block = 2 * ((place[PLACE_Y] + step) & (YS - 1)) + core

            @pl.when(chosen(block))
            def _():
                act(pltpu.make_async_copy(array, out(block), sem.at[n]))

    each(lambda copy: copy.start())
    return lambda: each(lambda copy: copy.wait())


def place_panel(place, tops, bottoms, chosen, out, sem):
    waits = [
        place_blocks(place, arrays, chosen, lambda block, rows=pl.ds(k * HALF, HALF): out(block, rows), sem.at[k])
        for k, arrays in enumerate((tops, bottoms))
    ]

    def wait():
        for one in waits:
            one()

    return wait


def eliminate(triangle, targets, store):
    for i in range(PARTS):
        value = product(halves(triangle[i, pl.ds(i * Q, Q), :]), halves(targets[i]))
        store(i, value)
        parts = halves(value)
        for k in range(i + 1, PARTS):
            targets[k] = targets[k] - product(halves(triangle[i, pl.ds(k * Q, Q), :]), parts)


def solve_kernel(place, rhs, *rest):
    tops, bottoms, rest = rest[: len(CHUNK)], rest[len(CHUNK) : 2 * len(CHUNK)], rest[2 * len(CHUNK) :]
    whole, two, three, triangle, rhs_buf, top_sem, bottom_sem, rhs_sem = rest

    @pl.when(place[ROW] == 0)
    def _():
        copy = pltpu.make_async_copy(rhs, rhs_buf, rhs_sem)
        copy.start()
        waits = [
            place_blocks(place, tops, lambda block: block < 2, lambda block: triangle.at[block, pl.ds(0, HALF)], top_sem),
            place_blocks(
                place, bottoms, lambda block: block < PARTS, lambda block: triangle.at[block, pl.ds(HALF, HALF)], bottom_sem
            ),
        ]
        for wait in waits:
            wait()
        copy.wait()

        def store(i, value):
            whole[pl.ds(i * Q, Q), :] = value
            if i >= 2:
                (two, three)[i - 2][...] = value

        eliminate(triangle, [rhs_buf[pl.ds(i * Q, Q), :] for i in range(PARTS)], store)


def solve(place, rhs, tops, bottoms):
    scratch = [
        pltpu.VMEM((PARTS, NB, Q), F32),
        pltpu.VMEM((NB, Q), F32),
        pltpu.SemaphoreType.DMA((COLS,)),
        pltpu.SemaphoreType.DMA((COLS,)),
        pltpu.SemaphoreType.DMA,
    ]
    shapes = [((NB, Q), F32), ((Q, Q), F32), ((Q, Q), F32)]
    return call(solve_kernel, "solve", shapes, scratch, (place, rhs, *tops, *bottoms))


def prepare_kernel(place, rhs, *rest):
    tops, bottoms, rest = rest[: len(CHUNK)], rest[len(CHUNK) : 2 * len(CHUNK)], rest[2 * len(CHUNK) :]
    w_high, w_low, y_out, triangle, left, targets, sem, left_sem, rhs_sem = rest

    @pl.when(place[ROW] == 1)
    def _():
        copy = pltpu.make_async_copy(rhs, targets.at[:, pl.ds(NB, Q)], rhs_sem)
        copy.start()
        waits = [
            place_panel(place, tops, bottoms, lambda b: b < PARTS, lambda b, rows: left.at[b, rows], left_sem),
            place_panel(place, tops, bottoms, lambda b: b >= PARTS, lambda b, rows: triangle.at[b - PARTS, rows], sem),
            copy.wait,
        ]
        for wait in waits:
            wait()
        for j in range(PARTS):
            targets[:, j * Q : (j + 1) * Q] = left[j]
        for i in range(PARTS):
            rows = pl.ds(i * Q, Q)
            value = product(halves(triangle[i, rows, :]), halves(targets[rows, :]))
            parts = halves(value)
            w_high[rows, :], w_low[rows, :] = parts[0][:, :NB], parts[1][:, :NB]
            y_out[rows, :] = value[:, NB:]
            for k in range(i + 1, PARTS):
                below = pl.ds(k * Q, Q)
                targets[below, :] -= product(halves(triangle[i, below, :]), parts)


def prepare(place, rhs, tops, bottoms):
    scratch = [
        pltpu.VMEM((PARTS, NB, Q), F32),
        pltpu.VMEM((PARTS, NB, Q), F32),
        pltpu.VMEM((NB, NB + Q), F32),
        pltpu.SemaphoreType.DMA((2, COLS)),
        pltpu.SemaphoreType.DMA((2, COLS)),
        pltpu.SemaphoreType.DMA,
    ]
    shapes = [((NB, NB), BF16)] * 2 + [((NB, Q), F32)]
    return call(prepare_kernel, "prepare", shapes, scratch, (place, rhs, *tops, *bottoms), vmem=32)


def combine_kernel(place, w_high, w_low, y_ref, first, *out):
    @pl.when(place[ROW] == 1)
    def _():
        solved = halves(first[...])
        for i in range(PARTS):
            rows = pl.ds(i * Q, Q)
            out[i][...] = y_ref[rows, :] - product((w_high[rows, :], w_low[rows, :]), solved)


def combine(place, w_high, w_low, y_value, first):
    vmem = [pl.BlockSpec(memory_space=pltpu.VMEM)] * 4
    operands = (place, w_high, w_low, y_value, first)
    return call(combine_kernel, "combine", [((Q, Q), F32)] * PARTS, [], operands, in_specs=vmem)


PIECES = ((0, Q), (Q, Q), (2 * Q, Q // 2), (2 * Q + Q // 2, Q // 2), (3 * Q, Q))


def update_kernel(base, slots, last, place, target, *rest):
    used = [n for n, (at, _) in enumerate(PIECES) if at // Q in slots]
    tops, bottoms, rest = rest[: len(CHUNK)], rest[len(CHUNK) : 2 * len(CHUNK)], rest[2 * len(CHUNK) :]
    pieces, rest = rest[: len(used)], rest[len(used) + int(base + len(slots) > PARTS) :]
    out, whole, blocks, target_buf, solved_buf, sem, target_sem, solved_sem, whole_sem = rest
    copies, kept = [], []
    for i, (n, piece) in enumerate(zip(used, pieces)):
        at, length = PIECES[n]
        here = pl.ds(slots.index(at // Q) * Q + at % Q, length)
        copies.append(pltpu.make_async_copy(piece, solved_buf.at[here], solved_sem.at[i]))
        start = pl.multiple_of(((at + place[TURN] * Q) & (NB - 1)) + base * Q, Q // 2)
        kept.append(pltpu.make_async_copy(solved_buf.at[here], whole.at[pl.ds(start, length)], whole_sem.at[i]))
    copies.append(pltpu.make_async_copy(target, target_buf, target_sem))

    def slot_of(block):
        return (block - place[TURN]) & (PARTS - 1)

    def chosen(block):
        here = (block >= base) & (block < base + PARTS)
        for slot in set(range(PARTS)) - set(slots):
            here &= slot_of(block) != slot
        return here

    def at_slot(block, rows):
        slot = slot_of(block)
        return blocks.at[jnp.where(slot > slots[-1], 0, sum(jnp.where(slot > other, 1, 0) for other in slots)), rows]

    wait_panel = place_panel(place, tops, bottoms, chosen, at_slot, sem)
    for copy in copies:
        copy.start()
    for copy in copies[: len(used)]:
        copy.wait()
    for copy in kept:
        copy.start()
    solved = [halves(solved_buf[pl.ds(i * Q, Q), :]) for i in range(len(slots))]
    for copy in copies[len(used) :]:
        copy.wait()
    wait_panel()
    for r in range(PARTS):
        rows = pl.ds(r * Q, Q)
        result = target_buf[rows, :]
        for i in range(len(slots)):
            result = result - product(halves(blocks[i, rows, :]), solved[i])
        out[rows, :] = jnp.where(place[ROW] >= 2, result, 0.0) if last else result
    for copy in kept:
        copy.wait()


def update(name, base, slots, last, place, target, tops, bottoms, pieces, *before):
    scratch = [
        pltpu.VMEM((len(slots), NB, Q), F32),
        pltpu.VMEM((NB, Q), F32),
        pltpu.VMEM((len(slots) * Q, Q), F32),
        pltpu.SemaphoreType.DMA((2, COLS)),
        pltpu.SemaphoreType.DMA,
        pltpu.SemaphoreType.DMA((len(pieces),)),
        pltpu.SemaphoreType.DMA((len(pieces),)),
    ]
    tops, bottoms = ([pltpu.with_memory_space_constraint(x, pltpu.HBM) for x in half] for half in (tops, bottoms))
    operands = (place, target, *tops, *bottoms, *pieces, *before)
    return call(
        functools.partial(update_kernel, base, slots, last),
        name,
        [((NB, Q), F32), ((2 * NB, Q), F32)],
        scratch,
        operands,
        out_specs=[pl.BlockSpec(memory_space=pltpu.VMEM), pl.BlockSpec(memory_space=pl.ANY)],
        input_output_aliases={len(operands) - 1: 1} if before else {},
        flops=(6 if before else UPDATE_COST) * NB * NB * Q,
    )


def along_z(moves):
    return [(a * XS + x, b * XS + x) for a, b in moves for x in range(XS)]


TO_NEXT = [(r, r // XS * XS + (r + 1) % XS) for r in range(ROWS)]
TO_LAST = [(b, a) for a, b in TO_NEXT]


def after(value, *others):
    return lax.optimization_barrier((value, *others))[0]


def scatter_first(two, three):
    relay = lax.ppermute(two, "row", [(0, 3)])
    return lax.ppermute(relay, "row", [(3, 2)]), lax.ppermute(three, "row", [(0, 3)])


def scatter_second(pieces):
    return [lax.ppermute(pieces[i], "row", [(1, (1 + i) % XS)]) for i in (1, 2, 3)]


def far_z(mine, z):
    near = lax.ppermute(mine, "row", along_z([(0, 3)]))
    far = lax.ppermute(mine, "row", along_z([(0, 5)]))
    return jnp.where(z == 0, mine, near + far)


def near_z(mine, z):
    up = lax.ppermute(mine, "row", along_z([(0, 1), (3, 4), (5, 6)]))
    down = lax.ppermute(mine, "row", along_z([(0, 7), (3, 2)]))
    return jnp.where((z == 0) | (z == 3) | (z == 5), mine, up + down)


def over_x(mine):
    return lax.ppermute(mine, "row", TO_LAST), lax.ppermute(mine, "row", TO_NEXT)


def across_x(after, before):
    return lax.ppermute(after[: Q // 2], "row", TO_LAST), lax.ppermute(before[Q // 2 :], "row", TO_NEXT)


def body(panel, rhs):
    row = lax.axis_index("row")
    col = lax.axis_index("col")
    z = row // XS

    def place(root):
        return jnp.stack([row, col // 2, col % 2, (row - root) % XS])

    def after(value, *others):
        return lax.optimization_barrier((value, *others))[0]

    top, bottom = payload(place(0), panel)
    top_near = near_chips(top, lambda r, y: r > 0 or y == 0)
    bottom_near = near_chips(bottom, lambda r, y: r > 0 or y <= 1)
    top_far = far_chip(top_near[0], None, lambda r, y: r > 0 or y == 0)
    bottom_far = far_chip(None, bottom_near[1], lambda r, y: r > 0 or y <= 1)
    tops = both_cores((top, *top_near, top_far))
    bottoms = both_cores((bottom, *bottom_near, bottom_far))

    first, two, three = solve(place(0), rhs, tops, bottoms)
    ahead = lax.ppermute(first, "row", [(0, 1)])
    two_ahead, three_ahead = scatter_first(two, three)
    w_high, w_low, y_value = prepare(place(0), rhs, tops, bottoms)
    mine_one = jnp.where(row == 1, ahead[Q : 2 * Q], two_ahead + three_ahead)
    mine_one = far_z(after(jnp.where(row == 0, first[:Q], mine_one), w_high), z)

    pieces = combine(place(0), w_high, w_low, y_value, ahead)
    got = scatter_second(pieces)
    mine_one = near_z(after(mine_one, *pieces), z)
    mine_two = jnp.where(row == 1, pieces[0], got[0] + got[1] + got[2])
    beside_one = over_x(after(mine_one, got[0]))
    across_one = across_x(*beside_one)
    mine_two = far_z(mine_two, z)
    pieces_one = [after(x, mine_two) for x in (mine_one, beside_one[0], *across_one, beside_one[1])]
    updated, whole = update("update", 0, (0, 1, 2, 3), False, place(0), rhs, tops, bottoms, pieces_one)
    mine_two = near_z(mine_two, z)
    beside_two = [after(piece, updated) for piece in over_x(mine_two)]
    across_two = across_x(*beside_two)
    pieces_two = (mine_two, *beside_two)
    updated, whole = update("most", PARTS, (0, 1, 3), False, place(1), updated, tops, bottoms, pieces_two, whole)
    return tuple(update("last", PARTS, (2,), True, place(1), updated, tops, bottoms, across_two, whole))


def solution(mesh):
    placed = (P("row", "col"), P("row", "col"))
    return jax.shard_map(
        body,
        mesh=mesh,
        in_specs=placed,
        out_specs=(P("row", "col"), P(None, "col")),
        check_vma=False,
    )
```

```python
import functools

import jax
import jax.numpy as jnp
from jax import lax
from jax.experimental import pallas as pl
from jax.experimental.pallas import tpu as pltpu
from jax.sharding import PartitionSpec as P

NB = 1024
HALF = NB // 2
Q = 256
PARTS = 4
XS = 4
YS = 4
ZS = 8
ROWS = XS * ZS
COLS = 2 * YS
F32 = jnp.float32
BF16 = jnp.bfloat16
BOTH = ("row", "col")
UPDATE_COST = 60


def halves(value):
    high = value.astype(BF16)
    return high, (value - high.astype(F32)).astype(BF16)


def product(left, right):
    dot = functools.partial(jnp.dot, preferred_element_type=F32)
    return dot(left[0], right[0]) + (dot(left[0], right[1]) + dot(left[1], right[0]))


def call(kernel, name, shapes, scratch, operands, in_specs=None, out_specs=None, vmem=24, flops=2 * NB * NB * Q, **options):
    operands = [pltpu.with_memory_space_constraint(x, pltpu.HBM) if x.ndim == 3 else x for x in operands]
    return pl.pallas_call(
        kernel,
        out_shape=[(pltpu.HBM if len(shape) == 3 else jax.ShapeDtypeStruct)(shape, dtype) for shape, dtype in shapes],
        in_specs=[pl.BlockSpec(memory_space=pltpu.SMEM)]
        + (in_specs or [pl.BlockSpec(memory_space=pl.ANY)] * (len(operands) - 1)),
        out_specs=out_specs or [pl.BlockSpec(memory_space=pltpu.VMEM)] * len(shapes),
        scratch_shapes=scratch,
        compiler_params=pltpu.CompilerParams(vmem_limit_bytes=vmem << 20),
        cost_estimate=pl.CostEstimate(flops=flops, bytes_accessed=8 << 20, transcendentals=0),
        name=name,
        **options,
    )(*operands)


ROW, PLACE_Y, CORE, TURN = range(4)


def payload_kernel(place, panel_ref, top_ref, bottom_ref):
    top_ref[...] = panel_ref[pl.ds(0, HALF), :]
    bottom_ref[...] = panel_ref[pl.ds(HALF, HALF), :]
    col = 2 * place[PLACE_Y] + place[CORE]
    number = col & (PARTS - 1)

    @pl.when(((place[ROW] == 0) & (col < PARTS)) | ((place[ROW] == 1) & (col >= PARTS)))
    def _():
        rows = lax.broadcasted_iota(jnp.int32, (Q, Q), 0)
        cols = lax.broadcasted_iota(jnp.int32, (Q, Q), 1)
        block = panel_ref[pl.ds(pl.multiple_of(number * Q, Q), Q), :]
        inverse = jnp.where(rows == cols, 1.0 / jnp.where(rows == cols, block, 1.0), 0.0)
        down, across = jnp.sum(inverse, axis=1, keepdims=True), jnp.sum(inverse, axis=0, keepdims=True)
        pair = ((rows >> 1) == (cols >> 1)) & (rows > cols)
        inverse = inverse - down * jnp.where(pair, block, 0.0) * across
        level = 1
        while (1 << level) < Q:
            pair = (rows >> (level + 1)) == (cols >> (level + 1))
            below = pair & (((rows >> level) & 1) == 1) & (((cols >> level) & 1) == 0)
            parts = halves(inverse)
            inner = product(halves(jnp.where(below, block, 0.0)), parts)
            inverse = inverse - product(parts, halves(inner))
            level += 1
        for i in range(PARTS):

            @pl.when(number == i)
            def _():
                half = (top_ref, bottom_ref)[i // 2]
                half[pl.ds((i % 2) * Q, Q), :] = inverse


def payload(place, panel):
    vmem = [pl.BlockSpec(memory_space=pltpu.VMEM)]
    return call(payload_kernel, "payload", [((HALF, Q), F32)] * 2, [], (place, panel), in_specs=vmem)


CHUNK = tuple((step, same) for step in (0, 1, 3, 2) for same in (True, False))


def pairs(step, origin, has):
    return [
        (r * COLS + 2 * y + k, r * COLS + 2 * ((y + step) % YS) + k)
        for r in range(ROWS)
        for y in range(YS)
        for k in (0, 1)
        if has(r, (y + origin) % YS)
    ]


def other_core(value):
    return lax.ppermute(value, "col", [(c, c ^ 1) for c in range(COLS)])


def near_chips(chunk, has):
    behind = lax.ppermute(chunk, BOTH, pairs(1, 0, has))
    return lax.ppermute(chunk, BOTH, pairs(-1, 0, has)), behind


def far_chip(ahead, behind, has):
    if behind is None:
        return lax.ppermute(ahead, BOTH, pairs(-1, 1, has))
    return lax.ppermute(behind, BOTH, pairs(1, -1, has))


def both_cores(values):
    return [x for value in values for x in (value, other_core(value))]


def place_blocks(place, arrays, chosen, out, sem):
    def each(act):
        for n, ((step, same), array) in enumerate(zip(CHUNK, arrays)):
            core = place[CORE] if same else 1 - place[CORE]
            block = 2 * ((place[PLACE_Y] + step) & (YS - 1)) + core

            @pl.when(chosen(block))
            def _():
                act(pltpu.make_async_copy(array, out(block), sem.at[n]))

    each(lambda copy: copy.start())
    return lambda: each(lambda copy: copy.wait())


def place_panel(place, tops, bottoms, chosen, out, sem):
    waits = [
        place_blocks(place, arrays, chosen, lambda block, rows=pl.ds(k * HALF, HALF): out(block, rows), sem.at[k])
        for k, arrays in enumerate((tops, bottoms))
    ]

    def wait():
        for one in waits:
            one()

    return wait


def eliminate(triangle, targets, store):
    for i in range(PARTS):
        value = product(halves(triangle[i, pl.ds(i * Q, Q), :]), halves(targets[i]))
        store(i, value)
        parts = halves(value)
        for k in range(i + 1, PARTS):
            targets[k] = targets[k] - product(halves(triangle[i, pl.ds(k * Q, Q), :]), parts)


def solve_kernel(place, rhs, *rest):
    tops, bottoms, rest = rest[: len(CHUNK)], rest[len(CHUNK) : 2 * len(CHUNK)], rest[2 * len(CHUNK) :]
    whole, two, three, triangle, rhs_buf, top_sem, bottom_sem, rhs_sem = rest

    @pl.when(place[ROW] == 0)
    def _():
        copy = pltpu.make_async_copy(rhs, rhs_buf, rhs_sem)
        copy.start()
        waits = [
            place_blocks(place, tops, lambda block: block < 2, lambda block: triangle.at[block, pl.ds(0, HALF)], top_sem),
            place_blocks(
                place, bottoms, lambda block: block < PARTS, lambda block: triangle.at[block, pl.ds(HALF, HALF)], bottom_sem
            ),
        ]
        for wait in waits:
            wait()
        copy.wait()

        def store(i, value):
            whole[pl.ds(i * Q, Q), :] = value
            if i >= 2:
                (two, three)[i - 2][...] = value

        eliminate(triangle, [rhs_buf[pl.ds(i * Q, Q), :] for i in range(PARTS)], store)


def solve(place, rhs, tops, bottoms):
    scratch = [
        pltpu.VMEM((PARTS, NB, Q), F32),
        pltpu.VMEM((NB, Q), F32),
        pltpu.SemaphoreType.DMA((COLS,)),
        pltpu.SemaphoreType.DMA((COLS,)),
        pltpu.SemaphoreType.DMA,
    ]
    shapes = [((NB, Q), F32), ((Q, Q), F32), ((Q, Q), F32)]
    return call(solve_kernel, "solve", shapes, scratch, (place, rhs, *tops, *bottoms))


def prepare_kernel(place, rhs, *rest):
    tops, bottoms, rest = rest[: len(CHUNK)], rest[len(CHUNK) : 2 * len(CHUNK)], rest[2 * len(CHUNK) :]
    w_high, w_low, y_out, triangle, left, targets, sem, left_sem, rhs_sem = rest

    @pl.when(place[ROW] == 1)
    def _():
        copy = pltpu.make_async_copy(rhs, targets.at[:, pl.ds(NB, Q)], rhs_sem)
        copy.start()
        waits = [
            place_panel(place, tops, bottoms, lambda b: b < PARTS, lambda b, rows: left.at[b, rows], left_sem),
            place_panel(place, tops, bottoms, lambda b: b >= PARTS, lambda b, rows: triangle.at[b - PARTS, rows], sem),
            copy.wait,
        ]
        for wait in waits:
            wait()
        for j in range(PARTS):
            targets[:, j * Q : (j + 1) * Q] = left[j]
        for i in range(PARTS):
            rows = pl.ds(i * Q, Q)
            value = product(halves(triangle[i, rows, :]), halves(targets[rows, :]))
            parts = halves(value)
            w_high[rows, :], w_low[rows, :] = parts[0][:, :NB], parts[1][:, :NB]
            y_out[rows, :] = value[:, NB:]
            for k in range(i + 1, PARTS):
                below = pl.ds(k * Q, Q)
                targets[below, :] -= product(halves(triangle[i, below, :]), parts)


def prepare(place, rhs, tops, bottoms):
    scratch = [
        pltpu.VMEM((PARTS, NB, Q), F32),
        pltpu.VMEM((PARTS, NB, Q), F32),
        pltpu.VMEM((NB, NB + Q), F32),
        pltpu.SemaphoreType.DMA((2, COLS)),
        pltpu.SemaphoreType.DMA((2, COLS)),
        pltpu.SemaphoreType.DMA,
    ]
    shapes = [((NB, NB), BF16)] * 2 + [((NB, Q), F32)]
    return call(prepare_kernel, "prepare", shapes, scratch, (place, rhs, *tops, *bottoms), vmem=32)


def combine_kernel(place, w_high, w_low, y_ref, first, *out):
    @pl.when(place[ROW] == 1)
    def _():
        solved = halves(first[...])
        for i in range(PARTS):
            rows = pl.ds(i * Q, Q)
            out[i][...] = y_ref[rows, :] - product((w_high[rows, :], w_low[rows, :]), solved)


def combine(place, w_high, w_low, y_value, first):
    vmem = [pl.BlockSpec(memory_space=pltpu.VMEM)] * 4
    operands = (place, w_high, w_low, y_value, first)
    return call(combine_kernel, "combine", [((Q, Q), F32)] * PARTS, [], operands, in_specs=vmem)


PIECES = ((0, Q), (Q, Q), (2 * Q, Q // 2), (2 * Q + Q // 2, Q // 2), (3 * Q, Q))


def turned(place, root):
    return (place[TURN] - root) & (PARTS - 1)


def piece_rows(place, root, at):
    return pl.multiple_of(((at + turned(place, root) * Q) & (NB - 1)) + root * NB, Q // 2)


def panel_blocks(place, root, slots, out):
    def slot_of(block):
        return (block - turned(place, root)) & (PARTS - 1)

    def chosen(block):
        here = (block >= root * PARTS) & (block < (root + 1) * PARTS)
        for slot in set(range(PARTS)) - set(slots):
            here &= slot_of(block) != slot
        return here

    return chosen, lambda block, rows: out(sum(jnp.where(slot_of(block) > other, 1, 0) for other in slots), rows)


def update_kernel(root, slots, ahead, place, target, *rest):
    tops, bottoms, rest = rest[: len(CHUNK)], rest[len(CHUNK) : 2 * len(CHUNK)], rest[2 * len(CHUNK) :]
    used = [(at, length) for at, length in PIECES if at // Q in slots]
    pieces, rest = rest[: len(used)], rest[len(used) + root :]
    out, whole, *rest = rest
    if ahead:
        (next_block, *rest) = rest
    blocks, target_buf, solved_buf, sem, target_sem, solved_sem, whole_sem = rest
    copies, kept = [], []
    for i, ((at, length), piece) in enumerate(zip(used, pieces)):
        here = pl.ds(slots.index(at // Q) * Q + at % Q, length)
        copies.append(pltpu.make_async_copy(piece, solved_buf.at[here], solved_sem.at[i]))
        there = whole.at[pl.ds(piece_rows(place, root, at), length)]
        kept.append(pltpu.make_async_copy(solved_buf.at[here], there, whole_sem.at[i]))
    copies.append(pltpu.make_async_copy(target, target_buf, target_sem))
    for copy in copies:
        copy.start()
    wait_panel = place_panel(
        place, tops, bottoms, *panel_blocks(place, root, slots, lambda n, rows: blocks.at[n, rows]), sem.at[0]
    )
    if ahead:
        chosen, there = panel_blocks(place, root, (ahead,), lambda _, rows: next_block.at[rows])
        wait_ahead = place_panel(place, tops, bottoms, chosen, there, sem.at[1])
    for copy in copies[: len(used)]:
        copy.wait()
    for copy in kept:
        copy.start()
    solved = [halves(solved_buf[pl.ds(i * Q, Q), :]) for i in range(len(slots))]
    copies[-1].wait()
    wait_panel()
    for r in range(PARTS):
        rows = pl.ds(r * Q, Q)
        result = target_buf[rows, :]
        for i in range(len(slots)):
            result = result - product(halves(blocks[i, rows, :]), solved[i])
        out[rows, :] = result
    if ahead:
        wait_ahead()
    for copy in kept:
        copy.wait()


def update(name, root, slots, ahead, place, target, tops, bottoms, pieces, *before):
    scratch = [
        pltpu.VMEM((len(slots), NB, Q), F32),
        pltpu.VMEM((NB, Q), F32),
        pltpu.VMEM((len(slots) * Q, Q), F32),
        pltpu.SemaphoreType.DMA((2, 2, COLS)),
        pltpu.SemaphoreType.DMA,
        pltpu.SemaphoreType.DMA((len(pieces),)),
        pltpu.SemaphoreType.DMA((len(pieces),)),
    ]
    tops, bottoms = ([pltpu.with_memory_space_constraint(x, pltpu.HBM) for x in half] for half in (tops, bottoms))
    operands = (place, target, *tops, *bottoms, *pieces, *before)
    vmem, anywhere = pl.BlockSpec(memory_space=pltpu.VMEM), pl.BlockSpec(memory_space=pl.ANY)
    return call(
        functools.partial(update_kernel, root, slots, ahead),
        name,
        [((NB, Q), F32), ((2 * NB, Q), F32)] + [((NB, Q), F32)] * bool(ahead),
        scratch,
        operands,
        out_specs=[vmem, anywhere] + [vmem] * bool(ahead),
        input_output_aliases={len(operands) - 1: 1} if before else {},
        flops=(6 if before else UPDATE_COST) * NB * NB * Q,
    )


def last_kernel(place, target, block, upper, lower, before, out, whole, sems):
    kept = []
    for i, (piece, at) in enumerate(((upper, 2 * Q), (lower, 2 * Q + Q // 2))):
        there = whole.at[pl.ds(piece_rows(place, 1, at), Q // 2)]
        kept.append(pltpu.make_async_copy(piece, there, sems.at[i]))
        kept[-1].start()
    solved = halves(jnp.concatenate([upper[...], lower[...]], axis=0))
    for r in range(PARTS):
        rows = pl.ds(r * Q, Q)
        result = target[rows, :] - product(halves(block[rows, :]), solved)
        out[rows, :] = jnp.where(place[ROW] >= 2, result, 0.0)
    for copy in kept:
        copy.wait()


def last(place, target, block, across, whole):
    vmem, anywhere = pl.BlockSpec(memory_space=pltpu.VMEM), pl.BlockSpec(memory_space=pl.ANY)
    return call(
        last_kernel,
        "last",
        [((NB, Q), F32), ((2 * NB, Q), F32)],
        [pltpu.SemaphoreType.DMA((2,))],
        (place, target, block, *across, whole),
        in_specs=[vmem] * 4 + [anywhere],
        out_specs=[vmem, anywhere],
        input_output_aliases={5: 1},
    )


def along_z(moves):
    return [(a * XS + x, b * XS + x) for a, b in moves for x in range(XS)]


TO_NEXT = [(r, r // XS * XS + (r + 1) % XS) for r in range(ROWS)]
TO_LAST = [(b, a) for a, b in TO_NEXT]


def after(value, *others):
    return lax.optimization_barrier((value, *others))[0]


def scatter_first(two, three):
    relay = lax.ppermute(two, "row", [(0, 3)])
    return lax.ppermute(relay, "row", [(3, 2)]), lax.ppermute(three, "row", [(0, 3)])


def scatter_second(pieces):
    return [lax.ppermute(pieces[i], "row", [(1, (1 + i) % XS)]) for i in (2, 3, 1)]


def far_z(mine, z):
    near = lax.ppermute(mine, "row", along_z([(0, 3)]))
    far = lax.ppermute(mine, "row", along_z([(0, 5)]))
    return jnp.where(z == 0, mine, near + far)


def near_z(mine, z):
    up = lax.ppermute(mine, "row", along_z([(0, 1), (3, 4), (5, 6)]))
    down = lax.ppermute(mine, "row", along_z([(0, 7), (3, 2)]))
    return jnp.where((z == 0) | (z == 3) | (z == 5), mine, up + down)


def over_x(mine):
    return lax.ppermute(mine, "row", TO_LAST), lax.ppermute(mine, "row", TO_NEXT)


def across_x(after, before):
    return lax.ppermute(after[: Q // 2], "row", TO_LAST), lax.ppermute(before[Q // 2 :], "row", TO_NEXT)


def body(panel, rhs):
    row = lax.axis_index("row")
    col = lax.axis_index("col")
    z = row // XS

    def place():
        return jnp.stack([row, col // 2, col % 2, row % XS])

    def after(value, *others):
        return lax.optimization_barrier((value, *others))[0]

    top, bottom = payload(place(), panel)
    top_near = near_chips(top, lambda r, y: r > 0 or y == 0)
    bottom_near = near_chips(bottom, lambda r, y: r > 0 or y <= 1)
    top_far = far_chip(top_near[0], None, lambda r, y: r > 0 or y == 0)
    bottom_far = far_chip(None, bottom_near[1], lambda r, y: r > 0 or y <= 1)
    tops = both_cores((top, *top_near, top_far))
    bottoms = both_cores((bottom, *bottom_near, bottom_far))

    first, two, three = solve(place(), rhs, tops, bottoms)
    ahead = lax.ppermute(first, "row", [(0, 1)])
    two_ahead, three_ahead = scatter_first(two, three)
    w_high, w_low, y_value = prepare(place(), rhs, tops, bottoms)
    mine_one = jnp.where(row == 1, ahead[Q : 2 * Q], two_ahead + three_ahead)
    mine_one = far_z(after(jnp.where(row == 0, first[:Q], mine_one), w_high), z)

    pieces = combine(place(), w_high, w_low, y_value, ahead)
    got = scatter_second(pieces)
    mine_one = near_z(after(mine_one, *pieces), z)
    mine_two = jnp.where(row == 1, pieces[0], got[0] + got[1] + got[2])
    beside_one = over_x(after(mine_one, got[0]))
    across_one = across_x(*beside_one)
    mine_two = far_z(mine_two, z)
    pieces_one = [after(x, mine_two) for x in (mine_one, beside_one[0], *across_one, beside_one[1])]
    mine_two = near_z(mine_two, z)
    updated, whole = update("update", 0, (0, 1, 2, 3), None, place(), rhs, tops, bottoms, pieces_one)
    beside_two = [after(piece, updated) for piece in over_x(mine_two)]
    across_two = across_x(*beside_two)
    pieces = (mine_two, *beside_two)
    updated, whole, block = update("most", 1, (0, 1, 3), 2, place(), updated, tops, bottoms, pieces, whole)
    return tuple(last(place(), updated, block, across_two, whole))


def solution(mesh):
    placed = (P("row", "col"), P("row", "col"))
    return jax.shard_map(
        body,
        mesh=mesh,
        in_specs=placed,
        out_specs=(P("row", "col"), P(None, "col")),
        check_vma=False,
    )
```

```python
import functools

import jax
import jax.numpy as jnp
from jax import lax
from jax.experimental import pallas as pl
from jax.experimental.pallas import tpu as pltpu
from jax.sharding import PartitionSpec as P

NB = 1024
HALF = NB // 2
Q = 256
PARTS = 4
XS = 4
YS = 4
ZS = 8
ROWS = XS * ZS
COLS = 2 * YS
F32 = jnp.float32
BF16 = jnp.bfloat16
BOTH = ("row", "col")
AROUND = 160
DIRECT = NB - 2 * AROUND
UPDATE_COST = 60


def halves(value):
    high = value.astype(BF16)
    return high, (value - high.astype(F32)).astype(BF16)


def product(left, right):
    dot = functools.partial(jnp.dot, preferred_element_type=F32)
    return dot(left[0], right[0]) + (dot(left[0], right[1]) + dot(left[1], right[0]))


def call(kernel, name, shapes, scratch, operands, in_specs=None, out_specs=None, vmem=24, flops=2 * NB * NB * Q, **options):
    operands = [pltpu.with_memory_space_constraint(x, pltpu.HBM) if x.ndim == 3 else x for x in operands]
    return pl.pallas_call(
        kernel,
        out_shape=[(pltpu.HBM if len(shape) == 3 else jax.ShapeDtypeStruct)(shape, dtype) for shape, dtype in shapes],
        in_specs=[pl.BlockSpec(memory_space=pltpu.SMEM)]
        + (in_specs or [pl.BlockSpec(memory_space=pl.ANY)] * (len(operands) - 1)),
        out_specs=out_specs or [pl.BlockSpec(memory_space=pltpu.VMEM)] * len(shapes),
        scratch_shapes=scratch,
        compiler_params=pltpu.CompilerParams(vmem_limit_bytes=vmem << 20),
        cost_estimate=pl.CostEstimate(flops=flops, bytes_accessed=8 << 20, transcendentals=0),
        name=name,
        **options,
    )(*operands)


ROW, PLACE_Y, CORE, TURN = range(4)


def payload_kernel(place, panel_ref, top_ref, bottom_ref):
    top_ref[...] = panel_ref[pl.ds(0, HALF), :]
    bottom_ref[...] = panel_ref[pl.ds(HALF, HALF), :]
    col = 2 * place[PLACE_Y] + place[CORE]
    number = col & (PARTS - 1)

    @pl.when(((place[ROW] == 0) & (col < PARTS)) | ((place[ROW] == 1) & (col >= PARTS)))
    def _():
        rows = lax.broadcasted_iota(jnp.int32, (Q, Q), 0)
        cols = lax.broadcasted_iota(jnp.int32, (Q, Q), 1)
        block = panel_ref[pl.ds(pl.multiple_of(number * Q, Q), Q), :]
        inverse = jnp.where(rows == cols, 1.0 / jnp.where(rows == cols, block, 1.0), 0.0)
        down, across = jnp.sum(inverse, axis=1, keepdims=True), jnp.sum(inverse, axis=0, keepdims=True)
        pair = ((rows >> 1) == (cols >> 1)) & (rows > cols)
        inverse = inverse - down * jnp.where(pair, block, 0.0) * across
        level = 1
        while (1 << level) < Q:
            pair = (rows >> (level + 1)) == (cols >> (level + 1))
            below = pair & (((rows >> level) & 1) == 1) & (((cols >> level) & 1) == 0)
            parts = halves(inverse)
            inner = product(halves(jnp.where(below, block, 0.0)), parts)
            inverse = inverse - product(parts, halves(inner))
            level += 1
        for i in range(PARTS):

            @pl.when(number == i)
            def _():
                half = (top_ref, bottom_ref)[i // 2]
                half[pl.ds((i % 2) * Q, Q), :] = inverse


def payload(place, panel):
    vmem = [pl.BlockSpec(memory_space=pltpu.VMEM)]
    return call(payload_kernel, "payload", [((HALF, Q), F32)] * 2, [], (place, panel), in_specs=vmem)


CHUNK = tuple((step, same) for step in (0, 1, 3, 2) for same in (True, False))


def pairs(step, origin, has):
    return [
        (r * COLS + 2 * y + k, r * COLS + 2 * ((y + step) % YS) + k)
        for r in range(ROWS)
        for y in range(YS)
        for k in (0, 1)
        if has(r, (y + origin) % YS)
    ]


def other_core(value):
    return lax.ppermute(value, "col", [(c, c ^ 1) for c in range(COLS)])


def near_chips(chunk, has):
    behind = lax.ppermute(chunk, BOTH, pairs(1, 0, has))
    return lax.ppermute(chunk, BOTH, pairs(-1, 0, has)), behind


def far_chip(ahead, behind, has):
    if behind is None:
        return lax.ppermute(ahead, BOTH, pairs(-1, 1, has))
    return lax.ppermute(behind, BOTH, pairs(1, -1, has))


def both_cores(values):
    return [x for value in values for x in (value, other_core(value))]


def place_blocks(place, arrays, chosen, out, sem):
    def each(act):
        for n, ((step, same), array) in enumerate(zip(CHUNK, arrays)):
            core = place[CORE] if same else 1 - place[CORE]
            block = 2 * ((place[PLACE_Y] + step) & (YS - 1)) + core

            @pl.when(chosen(block))
            def _():
                act(pltpu.make_async_copy(array, out(block), sem.at[n]))

    each(lambda copy: copy.start())
    return lambda: each(lambda copy: copy.wait())


def place_panel(place, tops, bottoms, chosen, out, sem):
    waits = [
        place_blocks(place, arrays, chosen, lambda block, rows=pl.ds(k * HALF, HALF): out(block, rows), sem.at[k])
        for k, arrays in enumerate((tops, bottoms))
    ]

    def wait():
        for one in waits:
            one()

    return wait


def eliminate(triangle, targets, store):
    for i in range(PARTS):
        value = product(halves(triangle[i, pl.ds(i * Q, Q), :]), halves(targets[i]))
        store(i, value)
        parts = halves(value)
        for k in range(i + 1, PARTS):
            targets[k] = targets[k] - product(halves(triangle[i, pl.ds(k * Q, Q), :]), parts)


def solve_kernel(place, rhs, *rest):
    tops, bottoms, rest = rest[: len(CHUNK)], rest[len(CHUNK) : 2 * len(CHUNK)], rest[2 * len(CHUNK) :]
    direct, up, down, two, three, triangle, rhs_buf, top_sem, bottom_sem, rhs_sem = rest

    @pl.when(place[ROW] == 0)
    def _():
        copy = pltpu.make_async_copy(rhs, rhs_buf, rhs_sem)
        copy.start()
        waits = [
            place_blocks(place, tops, lambda block: block < 2, lambda block: triangle.at[block, pl.ds(0, HALF)], top_sem),
            place_blocks(
                place, bottoms, lambda block: block < PARTS, lambda block: triangle.at[block, pl.ds(HALF, HALF)], bottom_sem
            ),
        ]
        for wait in waits:
            wait()
        copy.wait()

        def store(i, value):
            for array, start, count in ((direct, 0, DIRECT), (up, DIRECT, AROUND), (down, DIRECT + AROUND, AROUND)):
                low, high = max(start, i * Q), min(start + count, (i + 1) * Q)
                if low < high:
                    array[pl.ds(low - start, high - low), :] = value[low - i * Q : high - i * Q]
            if i >= 2:
                (two, three)[i - 2][...] = value

        eliminate(triangle, [rhs_buf[pl.ds(i * Q, Q), :] for i in range(PARTS)], store)


def solve(place, rhs, tops, bottoms):
    scratch = [
        pltpu.VMEM((PARTS, NB, Q), F32),
        pltpu.VMEM((NB, Q), F32),
        pltpu.SemaphoreType.DMA((COLS,)),
        pltpu.SemaphoreType.DMA((COLS,)),
        pltpu.SemaphoreType.DMA,
    ]
    shapes = [((rows, Q), F32) for rows in (DIRECT, AROUND, AROUND, Q, Q)]
    return call(solve_kernel, "solve", shapes, scratch, (place, rhs, *tops, *bottoms))


def prepare_kernel(place, rhs, *rest):
    tops, bottoms, rest = rest[: len(CHUNK)], rest[len(CHUNK) : 2 * len(CHUNK)], rest[2 * len(CHUNK) :]
    w_high, w_low, y_out, triangle, left, targets, sem, left_sem, rhs_sem = rest

    @pl.when(place[ROW] == 1)
    def _():
        copy = pltpu.make_async_copy(rhs, targets.at[:, pl.ds(NB, Q)], rhs_sem)
        copy.start()
        waits = [
            place_panel(place, tops, bottoms, lambda b: b < PARTS, lambda b, rows: left.at[b, rows], left_sem),
            place_panel(place, tops, bottoms, lambda b: b >= PARTS, lambda b, rows: triangle.at[b - PARTS, rows], sem),
            copy.wait,
        ]
        for wait in waits:
            wait()
        for j in range(PARTS):
            targets[:, j * Q : (j + 1) * Q] = left[j]
        for i in range(PARTS):
            rows = pl.ds(i * Q, Q)
            value = product(halves(triangle[i, rows, :]), halves(targets[rows, :]))
            parts = halves(value)
            w_high[rows, :], w_low[rows, :] = parts[0][:, :NB], parts[1][:, :NB]
            y_out[rows, :] = value[:, NB:]
            for k in range(i + 1, PARTS):
                below = pl.ds(k * Q, Q)
                targets[below, :] -= product(halves(triangle[i, below, :]), parts)


def prepare(place, rhs, tops, bottoms):
    scratch = [
        pltpu.VMEM((PARTS, NB, Q), F32),
        pltpu.VMEM((PARTS, NB, Q), F32),
        pltpu.VMEM((NB, NB + Q), F32),
        pltpu.SemaphoreType.DMA((2, COLS)),
        pltpu.SemaphoreType.DMA((2, COLS)),
        pltpu.SemaphoreType.DMA,
    ]
    shapes = [((NB, NB), BF16)] * 2 + [((NB, Q), F32)]
    held = [pltpu.with_memory_space_constraint(x, pltpu.HBM) for x in (*tops, *bottoms)]
    return call(prepare_kernel, "prepare", shapes, scratch, (place, rhs, *held), vmem=32)


def combine_kernel(place, w_high, w_low, y_ref, direct, up, down, *out):
    @pl.when(place[ROW] == 1)
    def _():
        solved = halves(jnp.concatenate([direct[...], up[...], down[...]], axis=0))
        for i in range(PARTS):
            rows = pl.ds(i * Q, Q)
            out[i][...] = y_ref[rows, :] - product((w_high[rows, :], w_low[rows, :]), solved)


def combine(place, w_high, w_low, y_value, *first):
    vmem = [pl.BlockSpec(memory_space=pltpu.VMEM)] * 6
    operands = (place, w_high, w_low, y_value, *first)
    return call(combine_kernel, "combine", [((Q, Q), F32)] * PARTS, [], operands, in_specs=vmem)


PIECES = ((0, Q), (Q, Q), (2 * Q, Q // 2), (2 * Q + Q // 2, Q // 2), (3 * Q, Q))


def turned(place, root):
    return (place[TURN] - root) & (PARTS - 1)


def piece_rows(place, root, at):
    return pl.multiple_of(((at + turned(place, root) * Q) & (NB - 1)) + root * NB, Q // 2)


def panel_blocks(place, root, slots, out):
    def slot_of(block):
        return (block - turned(place, root)) & (PARTS - 1)

    def chosen(block):
        here = (block >= root * PARTS) & (block < (root + 1) * PARTS)
        for slot in set(range(PARTS)) - set(slots):
            here &= slot_of(block) != slot
        return here

    return chosen, lambda block, rows: out(sum(jnp.where(slot_of(block) > other, 1, 0) for other in slots), rows)


def update_kernel(root, slots, ahead, place, target, *rest):
    tops, bottoms, rest = rest[: len(CHUNK)], rest[len(CHUNK) : 2 * len(CHUNK)], rest[2 * len(CHUNK) :]
    used = [(at, length) for at, length in PIECES if at // Q in slots]
    pieces, rest = rest[: len(used)], rest[len(used) + root :]
    out, whole, *rest = rest
    if ahead:
        (next_block, *rest) = rest
    blocks, target_buf, solved_buf, sem, target_sem, solved_sem, whole_sem = rest
    copies, kept = [], []
    for i, ((at, length), piece) in enumerate(zip(used, pieces)):
        here = pl.ds(slots.index(at // Q) * Q + at % Q, length)
        copies.append(pltpu.make_async_copy(piece, solved_buf.at[here], solved_sem.at[i]))
        there = whole.at[pl.ds(piece_rows(place, root, at), length)]
        kept.append(pltpu.make_async_copy(solved_buf.at[here], there, whole_sem.at[i]))
    copies.append(pltpu.make_async_copy(target, target_buf, target_sem))
    for copy in copies:
        copy.start()
    wait_panel = place_panel(
        place, tops, bottoms, *panel_blocks(place, root, slots, lambda n, rows: blocks.at[n, rows]), sem.at[0]
    )
    if ahead:
        chosen, there = panel_blocks(place, root, (ahead,), lambda _, rows: next_block.at[rows])
        wait_ahead = place_panel(place, tops, bottoms, chosen, there, sem.at[1])
    for copy in copies[: len(used)]:
        copy.wait()
    for copy in kept:
        copy.start()
    solved = [halves(solved_buf[pl.ds(i * Q, Q), :]) for i in range(len(slots))]
    copies[-1].wait()
    wait_panel()
    for r in range(PARTS):
        rows = pl.ds(r * Q, Q)
        result = target_buf[rows, :]
        for i in range(len(slots)):
            result = result - product(halves(blocks[i, rows, :]), solved[i])
        out[rows, :] = result
    if ahead:
        wait_ahead()
    for copy in kept:
        copy.wait()


def update(name, root, slots, ahead, place, target, tops, bottoms, pieces, *before):
    scratch = [
        pltpu.VMEM((len(slots), NB, Q), F32),
        pltpu.VMEM((NB, Q), F32),
        pltpu.VMEM((len(slots) * Q, Q), F32),
        pltpu.SemaphoreType.DMA((2, 2, COLS)),
        pltpu.SemaphoreType.DMA,
        pltpu.SemaphoreType.DMA((len(pieces),)),
        pltpu.SemaphoreType.DMA((len(pieces),)),
    ]
    tops, bottoms = ([pltpu.with_memory_space_constraint(x, pltpu.HBM) for x in half] for half in (tops, bottoms))
    operands = (place, target, *tops, *bottoms, *pieces, *before)
    vmem, anywhere = pl.BlockSpec(memory_space=pltpu.VMEM), pl.BlockSpec(memory_space=pl.ANY)
    return call(
        functools.partial(update_kernel, root, slots, ahead),
        name,
        [((NB, Q), F32), ((2 * NB, Q), F32)] + [((NB, Q), F32)] * bool(ahead),
        scratch,
        operands,
        out_specs=[vmem, anywhere] + [vmem] * bool(ahead),
        input_output_aliases={len(operands) - 1: 1} if before else {},
        flops=(6 if before else UPDATE_COST) * NB * NB * Q,
    )


def last_kernel(place, target, block, upper, lower, before, out, whole, sems):
    kept = []
    for i, (piece, at) in enumerate(((upper, 2 * Q), (lower, 2 * Q + Q // 2))):
        there = whole.at[pl.ds(piece_rows(place, 1, at), Q // 2)]
        kept.append(pltpu.make_async_copy(piece, there, sems.at[i]))
        kept[-1].start()
    solved = halves(jnp.concatenate([upper[...], lower[...]], axis=0))
    for r in range(PARTS):
        rows = pl.ds(r * Q, Q)
        result = target[rows, :] - product(halves(block[rows, :]), solved)
        out[rows, :] = jnp.where(place[ROW] >= 2, result, 0.0)
    for copy in kept:
        copy.wait()


def last(place, target, block, across, whole):
    vmem, anywhere = pl.BlockSpec(memory_space=pltpu.VMEM), pl.BlockSpec(memory_space=pl.ANY)
    return call(
        last_kernel,
        "last",
        [((NB, Q), F32), ((2 * NB, Q), F32)],
        [pltpu.SemaphoreType.DMA((2,))],
        (place, target, block, *across, whole),
        in_specs=[vmem] * 4 + [anywhere],
        out_specs=[vmem, anywhere],
        input_output_aliases={5: 1},
    )


def along_z(moves):
    return [(a * XS + x, b * XS + x) for a, b in moves for x in range(XS)]


TO_NEXT = [(r, r // XS * XS + (r + 1) % XS) for r in range(ROWS)]
TO_LAST = [(b, a) for a, b in TO_NEXT]


def after(value, *others):
    return lax.optimization_barrier((value, *others))[0]


def scatter_first(two, three):
    relay = lax.ppermute(two, "row", [(0, 3)])
    return lax.ppermute(relay, "row", [(3, 2)]), lax.ppermute(three, "row", [(0, 3)])


def scatter_second(pieces):
    return [lax.ppermute(pieces[i], "row", [(1, (1 + i) % XS)]) for i in (2, 3, 1)]


def far_z(mine, z):
    near = lax.ppermute(mine, "row", along_z([(0, 3)]))
    far = lax.ppermute(mine, "row", along_z([(0, 5)]))
    return jnp.where(z == 0, mine, near + far)


def near_z(mine, z):
    up = lax.ppermute(mine, "row", along_z([(0, 1), (3, 4), (5, 6)]))
    down = lax.ppermute(mine, "row", along_z([(0, 7), (3, 2)]))
    return jnp.where((z == 0) | (z == 3) | (z == 5), mine, up + down)


def over_x(mine):
    return lax.ppermute(mine, "row", TO_LAST), lax.ppermute(mine, "row", TO_NEXT)


def across_x(after, before):
    return lax.ppermute(after[: Q // 2], "row", TO_LAST), lax.ppermute(before[Q // 2 :], "row", TO_NEXT)


def body(panel, rhs):
    row = lax.axis_index("row")
    col = lax.axis_index("col")
    z = row // XS

    def place():
        return jnp.stack([row, col // 2, col % 2, row % XS])

    def after(value, *others):
        return lax.optimization_barrier((value, *others))[0]

    top, bottom = payload(place(), panel)
    top_near = near_chips(top, lambda r, y: r > 0 or y == 0)
    bottom_near = near_chips(bottom, lambda r, y: r > 0 or y <= 1)
    top_far = far_chip(top_near[0], None, lambda r, y: r > 0 or y == 0)
    bottom_far = far_chip(None, bottom_near[1], lambda r, y: r > 0 or y <= 1)
    tops = both_cores((top, *top_near, top_far))
    bottoms = both_cores((bottom, *bottom_near, bottom_far))

    first, up, down, two, three = solve(place(), rhs, tops, bottoms)
    last_z = (ZS - 1) * XS
    up = up_sent = lax.ppermute(up, "row", [(0, XS)])
    down = down_sent = lax.ppermute(down, "row", [(0, last_z)])
    for a, b in ((XS, XS + 1), (XS + 1, 1)):
        up = lax.ppermute(up, "row", [(a, b)])
    for a, b in ((last_z, last_z + 1), (last_z + 1, 1)):
        down = lax.ppermute(down, "row", [(a, b)])
    ahead = lax.ppermute(first, "row", [(0, 1)])
    two_ahead, three_ahead = scatter_first(after(two, down_sent), after(three, up_sent))
    w_high, w_low, y_value = prepare(place(), rhs, tops, bottoms)
    mine_one = jnp.where(row == 1, ahead[Q : 2 * Q], two_ahead + three_ahead)
    mine_one = far_z(after(jnp.where(row == 0, first[:Q], mine_one), w_high, up, down), z)

    pieces = combine(place(), w_high, w_low, y_value, ahead, up, down)
    got = scatter_second(pieces)
    mine_one = near_z(after(mine_one, *pieces), z)
    mine_two = jnp.where(row == 1, pieces[0], got[0] + got[1] + got[2])
    beside_one = over_x(after(mine_one, got[0]))
    across_one = across_x(*beside_one)
    mine_two = far_z(mine_two, z)
    pieces_one = [after(x, mine_two) for x in (mine_one, beside_one[0], *across_one, beside_one[1])]
    mine_two = near_z(mine_two, z)
    updated, whole = update("update", 0, (0, 1, 2, 3), None, place(), rhs, tops, bottoms, pieces_one)
    beside_two = [after(piece, updated) for piece in over_x(mine_two)]
    across_two = across_x(*beside_two)
    pieces = (mine_two, *beside_two)
    updated, whole, block = update("most", 1, (0, 1, 3), 2, place(), updated, tops, bottoms, pieces, whole)
    return tuple(last(place(), updated, block, across_two, whole))


def solution(mesh):
    placed = (P("row", "col"), P("row", "col"))
    return jax.shard_map(
        body,
        mesh=mesh,
        in_specs=placed,
        out_specs=(P("row", "col"), P(None, "col")),
        check_vma=False,
    )
```

```python
import functools

import jax
import jax.numpy as jnp
from jax import lax
from jax.experimental import pallas as pl
from jax.experimental.pallas import tpu as pltpu
from jax.sharding import PartitionSpec as P

NB = 1024
HALF = NB // 2
Q = 256
PARTS = 4
XS = 4
YS = 4
ZS = 8
ROWS = XS * ZS
COLS = 2 * YS
F32 = jnp.float32
BF16 = jnp.bfloat16
BOTH = ("row", "col")
AROUND = 96
DIRECT = NB - 2 * AROUND
UPDATE_COST = 60


def halves(value):
    high = value.astype(BF16)
    return high, (value - high.astype(F32)).astype(BF16)


def product(left, right):
    dot = functools.partial(jnp.dot, preferred_element_type=F32)
    return dot(left[0], right[0]) + (dot(left[0], right[1]) + dot(left[1], right[0]))


def call(kernel, name, shapes, scratch, operands, in_specs=None, out_specs=None, vmem=24, flops=2 * NB * NB * Q, **options):
    operands = [pltpu.with_memory_space_constraint(x, pltpu.HBM) if x.ndim == 3 else x for x in operands]
    return pl.pallas_call(
        kernel,
        out_shape=[(pltpu.HBM if len(shape) == 3 else jax.ShapeDtypeStruct)(shape, dtype) for shape, dtype in shapes],
        in_specs=[pl.BlockSpec(memory_space=pltpu.SMEM)]
        + (in_specs or [pl.BlockSpec(memory_space=pl.ANY)] * (len(operands) - 1)),
        out_specs=out_specs or [pl.BlockSpec(memory_space=pltpu.VMEM)] * len(shapes),
        scratch_shapes=scratch,
        compiler_params=pltpu.CompilerParams(vmem_limit_bytes=vmem << 20),
        cost_estimate=pl.CostEstimate(flops=flops, bytes_accessed=8 << 20, transcendentals=0),
        name=name,
        **options,
    )(*operands)


ROW, PLACE_Y, CORE, TURN = range(4)


def payload_kernel(place, panel_ref, top_ref, bottom_ref):
    top_ref[...] = panel_ref[pl.ds(0, HALF), :]
    bottom_ref[...] = panel_ref[pl.ds(HALF, HALF), :]
    col = 2 * place[PLACE_Y] + place[CORE]
    number = col & (PARTS - 1)

    @pl.when(((place[ROW] == 0) & (col < PARTS)) | ((place[ROW] == 1) & (col >= PARTS)))
    def _():
        rows = lax.broadcasted_iota(jnp.int32, (Q, Q), 0)
        cols = lax.broadcasted_iota(jnp.int32, (Q, Q), 1)
        block = panel_ref[pl.ds(pl.multiple_of(number * Q, Q), Q), :]
        inverse = jnp.where(rows == cols, 1.0 / jnp.where(rows == cols, block, 1.0), 0.0)
        down, across = jnp.sum(inverse, axis=1, keepdims=True), jnp.sum(inverse, axis=0, keepdims=True)
        pair = ((rows >> 1) == (cols >> 1)) & (rows > cols)
        inverse = inverse - down * jnp.where(pair, block, 0.0) * across
        level = 1
        while (1 << level) < Q:
            pair = (rows >> (level + 1)) == (cols >> (level + 1))
            below = pair & (((rows >> level) & 1) == 1) & (((cols >> level) & 1) == 0)
            parts = halves(inverse)
            inner = product(halves(jnp.where(below, block, 0.0)), parts)
            inverse = inverse - product(parts, halves(inner))
            level += 1
        for i in range(PARTS):

            @pl.when(number == i)
            def _():
                half = (top_ref, bottom_ref)[i // 2]
                half[pl.ds((i % 2) * Q, Q), :] = inverse


def payload(place, panel):
    vmem = [pl.BlockSpec(memory_space=pltpu.VMEM)]
    return call(payload_kernel, "payload", [((HALF, Q), F32)] * 2, [], (place, panel), in_specs=vmem)


CHUNK = tuple((step, same) for step in (0, 1, 3, 2) for same in (True, False))


def pairs(step, origin, has):
    return [
        (r * COLS + 2 * y + k, r * COLS + 2 * ((y + step) % YS) + k)
        for r in range(ROWS)
        for y in range(YS)
        for k in (0, 1)
        if has(r, (y + origin) % YS)
    ]


def other_core(value):
    return lax.ppermute(value, "col", [(c, c ^ 1) for c in range(COLS)])


def near_chips(chunk, has):
    behind = lax.ppermute(chunk, BOTH, pairs(1, 0, has))
    return lax.ppermute(chunk, BOTH, pairs(-1, 0, has)), behind


def far_chip(ahead, behind, has):
    if behind is None:
        return lax.ppermute(ahead, BOTH, pairs(-1, 1, has))
    return lax.ppermute(behind, BOTH, pairs(1, -1, has))


def both_cores(values):
    return [x for value in values for x in (value, other_core(value))]


def place_blocks(place, arrays, chosen, out, sem):
    def each(act):
        for n, ((step, same), array) in enumerate(zip(CHUNK, arrays)):
            core = place[CORE] if same else 1 - place[CORE]
            block = 2 * ((place[PLACE_Y] + step) & (YS - 1)) + core

            @pl.when(chosen(block))
            def _():
                act(pltpu.make_async_copy(array, out(block), sem.at[n]))

    each(lambda copy: copy.start())
    return lambda: each(lambda copy: copy.wait())


def place_panel(place, tops, bottoms, chosen, out, sem):
    waits = [
        place_blocks(place, arrays, chosen, lambda block, rows=pl.ds(k * HALF, HALF): out(block, rows), sem.at[k])
        for k, arrays in enumerate((tops, bottoms))
    ]

    def wait():
        for one in waits:
            one()

    return wait


def eliminate(triangle, targets, store):
    for i in range(PARTS):
        value = product(halves(triangle[i, pl.ds(i * Q, Q), :]), halves(targets[i]))
        store(i, value)
        parts = halves(value)
        for k in range(i + 1, PARTS):
            targets[k] = targets[k] - product(halves(triangle[i, pl.ds(k * Q, Q), :]), parts)


def solve_kernel(place, rhs, *rest):
    tops, bottoms, rest = rest[: len(CHUNK)], rest[len(CHUNK) : 2 * len(CHUNK)], rest[2 * len(CHUNK) :]
    direct, up, down, two, three, triangle, rhs_buf, top_sem, bottom_sem, rhs_sem = rest

    @pl.when(place[ROW] == 0)
    def _():
        copy = pltpu.make_async_copy(rhs, rhs_buf, rhs_sem)
        copy.start()
        waits = [
            place_blocks(place, tops, lambda block: block < 2, lambda block: triangle.at[block, pl.ds(0, HALF)], top_sem),
            place_blocks(
                place, bottoms, lambda block: block < PARTS, lambda block: triangle.at[block, pl.ds(HALF, HALF)], bottom_sem
            ),
        ]
        for wait in waits:
            wait()
        copy.wait()

        def store(i, value):
            for array, start, count in ((direct, 0, DIRECT), (up, DIRECT, AROUND), (down, DIRECT + AROUND, AROUND)):
                low, high = max(start, i * Q), min(start + count, (i + 1) * Q)
                if low < high:
                    array[pl.ds(low - start, high - low), :] = value[low - i * Q : high - i * Q]
            if i >= 2:
                (two, three)[i - 2][...] = value

        eliminate(triangle, [rhs_buf[pl.ds(i * Q, Q), :] for i in range(PARTS)], store)


def solve(place, rhs, tops, bottoms):
    scratch = [
        pltpu.VMEM((PARTS, NB, Q), F32),
        pltpu.VMEM((NB, Q), F32),
        pltpu.SemaphoreType.DMA((COLS,)),
        pltpu.SemaphoreType.DMA((COLS,)),
        pltpu.SemaphoreType.DMA,
    ]
    shapes = [((rows, Q), F32) for rows in (DIRECT, AROUND, AROUND, Q, Q)]
    return call(solve_kernel, "solve", shapes, scratch, (place, rhs, *tops, *bottoms))


def prepare_kernel(place, rhs, *rest):
    tops, bottoms, rest = rest[: len(CHUNK)], rest[len(CHUNK) : 2 * len(CHUNK)], rest[2 * len(CHUNK) :]
    w_high, w_low, y_out, triangle, left, targets, sem, left_sem, rhs_sem = rest

    @pl.when(place[ROW] == 1)
    def _():
        copy = pltpu.make_async_copy(rhs, targets.at[:, pl.ds(NB, Q)], rhs_sem)
        copy.start()
        waits = [
            place_panel(place, tops, bottoms, lambda b: b < PARTS, lambda b, rows: left.at[b, rows], left_sem),
            place_panel(place, tops, bottoms, lambda b: b >= PARTS, lambda b, rows: triangle.at[b - PARTS, rows], sem),
            copy.wait,
        ]
        for wait in waits:
            wait()
        for j in range(PARTS):
            targets[:, j * Q : (j + 1) * Q] = left[j]
        for i in range(PARTS):
            rows = pl.ds(i * Q, Q)
            value = product(halves(triangle[i, rows, :]), halves(targets[rows, :]))
            parts = halves(value)
            w_high[rows, :], w_low[rows, :] = parts[0][:, :NB], parts[1][:, :NB]
            y_out[rows, :] = value[:, NB:]
            for k in range(i + 1, PARTS):
                below = pl.ds(k * Q, Q)
                targets[below, :] -= product(halves(triangle[i, below, :]), parts)


def prepare(place, rhs, tops, bottoms):
    scratch = [
        pltpu.VMEM((PARTS, NB, Q), F32),
        pltpu.VMEM((PARTS, NB, Q), F32),
        pltpu.VMEM((NB, NB + Q), F32),
        pltpu.SemaphoreType.DMA((2, COLS)),
        pltpu.SemaphoreType.DMA((2, COLS)),
        pltpu.SemaphoreType.DMA,
    ]
    shapes = [((NB, NB), BF16)] * 2 + [((NB, Q), F32)]
    held = [pltpu.with_memory_space_constraint(x, pltpu.HBM) for x in (*tops, *bottoms)]
    return call(prepare_kernel, "prepare", shapes, scratch, (place, rhs, *held), vmem=32)


def combine_kernel(place, w_high, w_low, y_ref, direct, up, down, *out):
    @pl.when(place[ROW] == 1)
    def _():
        solved = halves(jnp.concatenate([direct[...], up[...], down[...]], axis=0))
        for i in range(PARTS):
            rows = pl.ds(i * Q, Q)
            out[i][...] = y_ref[rows, :] - product((w_high[rows, :], w_low[rows, :]), solved)


def combine(place, w_high, w_low, y_value, *first):
    vmem = [pl.BlockSpec(memory_space=pltpu.VMEM)] * 6
    operands = (place, w_high, w_low, y_value, *first)
    return call(combine_kernel, "combine", [((Q, Q), F32)] * PARTS, [], operands, in_specs=vmem)


PIECES = ((0, Q), (Q, Q), (2 * Q, Q // 2), (2 * Q + Q // 2, Q // 2), (3 * Q, Q))


def turned(place, root):
    return (place[TURN] - root) & (PARTS - 1)


def piece_rows(place, root, at):
    return pl.multiple_of(((at + turned(place, root) * Q) & (NB - 1)) + root * NB, Q // 2)


def panel_blocks(place, root, slots, out):
    def slot_of(block):
        return (block - turned(place, root)) & (PARTS - 1)

    def chosen(block):
        here = (block >= root * PARTS) & (block < (root + 1) * PARTS)
        for slot in set(range(PARTS)) - set(slots):
            here &= slot_of(block) != slot
        return here

    return chosen, lambda block, rows: out(sum(jnp.where(slot_of(block) > other, 1, 0) for other in slots), rows)


def update_kernel(root, slots, ahead, place, target, *rest):
    tops, bottoms, rest = rest[: len(CHUNK)], rest[len(CHUNK) : 2 * len(CHUNK)], rest[2 * len(CHUNK) :]
    used = [(at, length) for at, length in PIECES if at // Q in slots]
    pieces, rest = rest[: len(used)], rest[len(used) + root :]
    out, whole, *rest = rest
    if ahead:
        (next_block, *rest) = rest
    blocks, target_buf, solved_buf, sem, target_sem, solved_sem, whole_sem = rest
    copies, kept = [], []
    for i, ((at, length), piece) in enumerate(zip(used, pieces)):
        here = pl.ds(slots.index(at // Q) * Q + at % Q, length)
        copies.append(pltpu.make_async_copy(piece, solved_buf.at[here], solved_sem.at[i]))
        there = whole.at[pl.ds(piece_rows(place, root, at), length)]
        kept.append(pltpu.make_async_copy(solved_buf.at[here], there, whole_sem.at[i]))
    copies.append(pltpu.make_async_copy(target, target_buf, target_sem))
    for copy in copies:
        copy.start()
    wait_panel = place_panel(
        place, tops, bottoms, *panel_blocks(place, root, slots, lambda n, rows: blocks.at[n, rows]), sem.at[0]
    )
    if ahead:
        chosen, there = panel_blocks(place, root, (ahead,), lambda _, rows: next_block.at[rows])
        wait_ahead = place_panel(place, tops, bottoms, chosen, there, sem.at[1])
    for copy in copies[: len(used)]:
        copy.wait()
    for copy in kept:
        copy.start()
    solved = [halves(solved_buf[pl.ds(i * Q, Q), :]) for i in range(len(slots))]
    copies[-1].wait()
    wait_panel()
    for r in range(PARTS):
        rows = pl.ds(r * Q, Q)
        result = target_buf[rows, :]
        for i in range(len(slots)):
            result = result - product(halves(blocks[i, rows, :]), solved[i])
        out[rows, :] = result
    if ahead:
        wait_ahead()
    for copy in kept:
        copy.wait()


def update(name, root, slots, ahead, place, target, tops, bottoms, pieces, *before):
    scratch = [
        pltpu.VMEM((len(slots), NB, Q), F32),
        pltpu.VMEM((NB, Q), F32),
        pltpu.VMEM((len(slots) * Q, Q), F32),
        pltpu.SemaphoreType.DMA((2, 2, COLS)),
        pltpu.SemaphoreType.DMA,
        pltpu.SemaphoreType.DMA((len(pieces),)),
        pltpu.SemaphoreType.DMA((len(pieces),)),
    ]
    tops, bottoms = ([pltpu.with_memory_space_constraint(x, pltpu.HBM) for x in half] for half in (tops, bottoms))
    operands = (place, target, *tops, *bottoms, *pieces, *before)
    vmem, anywhere = pl.BlockSpec(memory_space=pltpu.VMEM), pl.BlockSpec(memory_space=pl.ANY)
    return call(
        functools.partial(update_kernel, root, slots, ahead),
        name,
        [((NB, Q), F32), ((2 * NB, Q), F32)] + [((NB, Q), F32)] * bool(ahead),
        scratch,
        operands,
        out_specs=[vmem, anywhere] + [vmem] * bool(ahead),
        input_output_aliases={len(operands) - 1: 1} if before else {},
        flops=(6 if before else UPDATE_COST) * NB * NB * Q,
    )


def last_kernel(place, target, block, upper, lower, before, out, whole, sems):
    kept = []
    for i, (piece, at) in enumerate(((upper, 2 * Q), (lower, 2 * Q + Q // 2))):
        there = whole.at[pl.ds(piece_rows(place, 1, at), Q // 2)]
        kept.append(pltpu.make_async_copy(piece, there, sems.at[i]))
        kept[-1].start()
    solved = halves(jnp.concatenate([upper[...], lower[...]], axis=0))
    for r in range(PARTS):
        rows = pl.ds(r * Q, Q)
        result = target[rows, :] - product(halves(block[rows, :]), solved)
        out[rows, :] = jnp.where(place[ROW] >= 2, result, 0.0)
    for copy in kept:
        copy.wait()


def last(place, target, block, across, whole):
    vmem, anywhere = pl.BlockSpec(memory_space=pltpu.VMEM), pl.BlockSpec(memory_space=pl.ANY)
    return call(
        last_kernel,
        "last",
        [((NB, Q), F32), ((2 * NB, Q), F32)],
        [pltpu.SemaphoreType.DMA((2,))],
        (place, target, block, *across, whole),
        in_specs=[vmem] * 4 + [anywhere],
        out_specs=[vmem, anywhere],
        input_output_aliases={5: 1},
    )


def along_z(moves):
    return [(a * XS + x, b * XS + x) for a, b in moves for x in range(XS)]


TO_NEXT = [(r, r // XS * XS + (r + 1) % XS) for r in range(ROWS)]
TO_LAST = [(b, a) for a, b in TO_NEXT]


def after(value, *others):
    return lax.optimization_barrier((value, *others))[0]


def scatter_first(two, three):
    relay = lax.ppermute(two, "row", [(0, 3)])
    return lax.ppermute(relay, "row", [(3, 2)]), lax.ppermute(three, "row", [(0, 3)])


def scatter_second(pieces):
    return [lax.ppermute(pieces[i], "row", [(1, (1 + i) % XS)]) for i in (2, 3, 1)]


def far_z(mine, z):
    near = lax.ppermute(mine, "row", along_z([(0, 3)]))
    far = lax.ppermute(mine, "row", along_z([(0, 5)]))
    return jnp.where(z == 0, mine, near + far)


def near_z(mine, z):
    up = lax.ppermute(mine, "row", along_z([(0, 1), (3, 4), (5, 6)]))
    down = lax.ppermute(mine, "row", along_z([(0, 7), (3, 2)]))
    return jnp.where((z == 0) | (z == 3) | (z == 5), mine, up + down)


def over_x(mine):
    return lax.ppermute(mine, "row", TO_LAST), lax.ppermute(mine, "row", TO_NEXT)


def across_x(after, before):
    return lax.ppermute(after[: Q // 2], "row", TO_LAST), lax.ppermute(before[Q // 2 :], "row", TO_NEXT)


def body(panel, rhs):
    row = lax.axis_index("row")
    col = lax.axis_index("col")
    z = row // XS

    def place():
        return jnp.stack([row, col // 2, col % 2, row % XS])

    def after(value, *others):
        return lax.optimization_barrier((value, *others))[0]

    top, bottom = payload(place(), panel)
    top_near = near_chips(top, lambda r, y: r > 0 or y == 0)
    bottom_near = near_chips(bottom, lambda r, y: r > 0 or y <= 1)
    top_far = far_chip(top_near[0], None, lambda r, y: r > 0 or y == 0)
    bottom_far = far_chip(None, bottom_near[1], lambda r, y: r > 0 or y <= 1)
    tops = both_cores((top, *top_near, top_far))
    bottoms = both_cores((bottom, *bottom_near, bottom_far))

    first, up, down, two, three = solve(place(), rhs, tops, bottoms)
    last_z = (ZS - 1) * XS
    up = up_sent = lax.ppermute(up, "row", [(0, XS)])
    down = down_sent = lax.ppermute(down, "row", [(0, last_z)])
    for a, b in ((XS, XS + 1), (XS + 1, 1)):
        up = lax.ppermute(up, "row", [(a, b)])
    for a, b in ((last_z, last_z + 1), (last_z + 1, 1)):
        down = lax.ppermute(down, "row", [(a, b)])
    ahead = lax.ppermute(first, "row", [(0, 1)])
    two_ahead, three_ahead = scatter_first(after(two, down_sent), after(three, up_sent))
    w_high, w_low, y_value = prepare(place(), rhs, tops, bottoms)
    mine_one = jnp.where(row == 1, ahead[Q : 2 * Q], two_ahead + three_ahead)
    mine_one = far_z(after(jnp.where(row == 0, first[:Q], mine_one), w_high, up, down), z)

    pieces = combine(place(), w_high, w_low, y_value, ahead, up, down)
    got = scatter_second(pieces)
    mine_one = near_z(after(mine_one, *pieces), z)
    mine_two = jnp.where(row == 1, pieces[0], got[0] + got[1] + got[2])
    beside_one = over_x(after(mine_one, got[0]))
    across_one = across_x(*beside_one)
    mine_two = far_z(mine_two, z)
    pieces_one = [after(x, mine_two) for x in (mine_one, beside_one[0], *across_one, beside_one[1])]
    mine_two = near_z(mine_two, z)
    updated, whole = update("update", 0, (0, 1, 2, 3), None, place(), rhs, tops, bottoms, pieces_one)
    beside_two = [after(piece, updated) for piece in over_x(mine_two)]
    across_two = across_x(*beside_two)
    pieces = (mine_two, *beside_two)
    updated, whole, block = update("most", 1, (0, 1, 3), 2, place(), updated, tops, bottoms, pieces, whole)
    return tuple(last(place(), updated, block, across_two, whole))


def solution(mesh):
    placed = (P("row", "col"), P("row", "col"))
    return jax.shard_map(
        body,
        mesh=mesh,
        in_specs=placed,
        out_specs=(P("row", "col"), P(None, "col")),
        check_vma=False,
    )
```
